32 devices in a mesh: rep: 8 (over y, x, core), tp: 4 (over z).
Axes of the slice: x: 2, y: 2, z: 4, core: 2. Of those that a mesh axis runs over, the one named last changes fastest.
Arguments:
- inputs: bfloat16 [4, 512, 5120], P(None, 'rep'), may hold values from -6 to 6
- qkv_weight: bfloat16 [2, 5120, 6144], P(None, ('rep', 'tp')), may hold values from -0.078125 to 0.078125
- out_weight: bfloat16 [2, 5120, 4096], P(None, ('rep', 'tp')), may hold values from -0.25 to 0.25
- norm_gain: float32 [2, 5120], replicated, may hold values from 0.1 to 1.9
- query_gain: float32 [2, 128], replicated, may hold values from 0.5 to 2
- key_gain: float32 [2, 128], replicated, may hold values from 0.5 to 2
- stored_rotated_keys: bfloat16 [2, 512, 8, 256, 128], P(None, 'rep', 'tp'), may hold values from -540 to 540
- stored_cache_values: bfloat16 [2, 512, 8, 256, 128], P(None, 'rep', 'tp'), may hold values from -6 to 6
- lengths: int32 [512], P('rep'), may hold values from 1 to 256, as said below
Outputs:
- final_hidden: bfloat16 [4, 512, 5120], P(None, 'rep')
The draws below stay inside these ranges and needn't reach their ends.
Inputs may be any that keep to these rules, and one draw needn't show every extreme that they name: `lengths`: in every replica some row has exactly 256 cached positions.
All inputs are finite; a program needn't handle non-finite values.
Results may differ from the reference program's by a relative error of at most 0.039.
The reference program's roundings to bfloat16 on the way count: a program that leaves them out, or rounds other values in their place, can miss the bound.
Values may be sent and summed in bfloat16 or wider, within the bound.
No kernel may reach another device: no remote copies, remote signals or barrier semaphores. Data moves between devices by JAX's collectives and lax.ppermute only.
A program may use at most 192 MiB of HBM per device.

```python
import math
import jax
import jax.numpy as jnp
from jax import lax

D = 5120
KEY_VALUE_HEADS = 8
HEAD_SIZE = 128
HQ = 32
LAYER_COUNT = 2
STEPS = 4
REPLICA_ROWS = 64
CACHE_SLOTS = 256
REPLICA_ROW_TOTAL = 512
QKV = 6144
N_REP = 8


def draw_stored_rotated_keys(key, part):
    key = jax.random.fold_in(key, 11)
    leading_shape, trailing_shape = jax.random.split(key)
    maximum_score = math.log(4.0)
    scale_factors = jnp.exp(jax.random.uniform(leading_shape, (LAYER_COUNT, REPLICA_ROW_TOTAL, KEY_VALUE_HEADS, 1, 1), jnp.float32, 0.0, maximum_score))
    value_rows = jax.random.truncated_normal(trailing_shape, -6.0, 6.0, (LAYER_COUNT, REPLICA_ROW_TOTAL, KEY_VALUE_HEADS, CACHE_SLOTS, HEAD_SIZE), jnp.float32)
    return (value_rows * scale_factors).astype(jnp.bfloat16)


def draw_lengths(key, part):
    key = jax.random.fold_in(key, 5)
    leading_shape, trailing_shape = jax.random.split(key)
    drawn = jax.random.randint(leading_shape, (REPLICA_ROW_TOTAL,), 1, CACHE_SLOTS + 1)
    offsets = jax.random.randint(trailing_shape, (REPLICA_ROW_TOTAL // REPLICA_ROWS, 1), 0, REPLICA_ROWS)
    filled = jnp.arange(REPLICA_ROWS, dtype=jnp.int32)[None, :] == offsets
    return jnp.where(filled.reshape(REPLICA_ROW_TOTAL), CACHE_SLOTS, drawn).astype(jnp.int32)


def levels(own_key, shape, shards, least, largest):
    factor_of, own = 1.0, jax.random.fold_in(own_key, 6)
    for dim, parts in shards:
        draws = jnp.exp(jax.random.uniform(jax.random.fold_in(own, dim), (parts,), jnp.float32, least / len(shards), largest / len(shards)))
        factor_of = factor_of * jnp.repeat(draws, shape[dim] // parts).reshape([-1 if axis == dim else 1 for axis in range(len(shape))])
    return factor_of


def gaussian(stream_key, extent, deviation, reach, pieces=(), held_as=jnp.bfloat16):
    loudness = levels(stream_key, extent, pieces, -0.22, 0.18) if pieces else 1.0
    values = jax.random.normal(stream_key, extent, jnp.float32) * deviation * loudness
    return jnp.minimum(jnp.maximum(values, -reach), reach).astype(held_as)


def setup_inputs(seed: int = 0) -> dict:
    seeds = jax.random.split(jax.random.key(seed), 10)
    return {
        "inputs": gaussian(seeds[0], (STEPS, REPLICA_ROW_TOTAL, D), 1.0, 6.0, ((1, 8),)),
        "qkv_weight": gaussian(seeds[1], (LAYER_COUNT, D, QKV), D ** -0.5, 0.078125, ((1, 32),)),
        "out_weight": gaussian(seeds[2], (LAYER_COUNT, D, HQ * HEAD_SIZE), (HQ * HEAD_SIZE // 8) ** -0.5, 0.25, ((1, 32),)),
        "norm_gain": jnp.clip(1.0 + 0.18 * jax.random.normal(seeds[3], (LAYER_COUNT, D), jnp.float32), 0.1, 1.9),
        "query_gain": jnp.clip(jnp.exp(jax.random.uniform(seeds[4], (LAYER_COUNT, HEAD_SIZE), jnp.float32, math.log(0.5), math.log(2.0))), 0.5, 2.0),
        "key_gain": jnp.clip(jnp.exp(jax.random.uniform(seeds[5], (LAYER_COUNT, HEAD_SIZE), jnp.float32, math.log(0.5), math.log(2.0))), 0.5, 2.0),
        "stored_rotated_keys": draw_stored_rotated_keys(jax.random.fold_in(seeds[9], 71), 0),
        "stored_cache_values": gaussian(seeds[7], (LAYER_COUNT, REPLICA_ROW_TOTAL, KEY_VALUE_HEADS, CACHE_SLOTS, HEAD_SIZE), 1.0, 6.0, ((1, 8), (2, 4))),
        "lengths": draw_lengths(jax.random.fold_in(seeds[9], 71), 0),
    }


epsilon = 1e-06
rope_base = 1000000.0

def rms_scale(value_rows, gain):
    wide = value_rows.astype(jnp.float32)
    return wide * lax.rsqrt(lax.optimization_barrier(jnp.mean(wide * wide, axis=-1, keepdims=True)) + epsilon) * gain

def rotate(value_rows, positions):
    half_dim = value_rows.shape[-1] // 2
    frequency = rope_base ** (-jnp.arange(half_dim, dtype=jnp.float32) / half_dim)
    angles = positions.astype(jnp.float32)[..., None] * frequency
    cosine = jnp.cos(angles)
    sine = jnp.sin(angles)
    leading_shape = value_rows[..., :half_dim]
    trailing_shape = value_rows[..., half_dim:]
    return jnp.concatenate([leading_shape * cosine - trailing_shape * sine, trailing_shape * cosine + leading_shape * sine], axis=-1)

def attend(queries, new_keys, new_values, old_keys, old_values, lengths):
    step_count = queries.shape[0]
    head_dim = queries.shape[-1]
    slots = old_keys.shape[2]
    queries_wide = queries.astype(jnp.float32)
    score_old = jnp.einsum('srkgd,rkcd->srkgc', queries_wide, old_keys.astype(jnp.float32)) * head_dim ** (-0.5)
    score_new = jnp.einsum('srkgd,trkd->srkgt', queries_wide, new_keys.astype(jnp.float32)) * head_dim ** (-0.5)
    live = jnp.arange(slots, dtype=jnp.int32)[None, :] < lengths[:, None]
    score_old = jnp.where(live[None, :, None, None, :], score_old, -jnp.inf)
    order = jnp.arange(step_count, dtype=jnp.int32)
    causal = order[None, :] <= order[:, None]
    score_new = jnp.where(causal[:, None, None, None, :], score_new, -jnp.inf)
    highest = jnp.maximum(lax.optimization_barrier(jnp.max(score_old, axis=-1)), lax.optimization_barrier(jnp.max(score_new, axis=-1)))[..., None]
    weight_old = jnp.exp(score_old - highest)
    weight_new = jnp.exp(score_new - highest)
    denominator = lax.optimization_barrier(jnp.sum(weight_old, axis=-1, keepdims=True)) + lax.optimization_barrier(jnp.sum(weight_new, axis=-1, keepdims=True))
    share_old = (weight_old / denominator).astype(jnp.bfloat16)
    share_new = (weight_new / denominator).astype(jnp.bfloat16)
    mixed = jnp.einsum('srkgc,rkcd->srkgd', share_old.astype(jnp.float32), old_values.astype(jnp.float32))
    mixed = mixed + jnp.einsum('srkgt,trkd->srkgd', share_new.astype(jnp.float32), new_values.astype(jnp.float32))
    return mixed.astype(jnp.bfloat16)

def decode_replica(hidden, old_keys, old_values, lengths, qkv_weight, out_weight, norm_gain, query_gain, key_gain):
    step_count = hidden.shape[0]
    row_count = hidden.shape[1]
    model_width = hidden.shape[2]
    groups = old_keys.shape[2]
    head_dim = old_keys.shape[4]
    per_group = qkv_weight.shape[2] // (groups * head_dim)
    positions = lengths[None, :] + jnp.arange(step_count, dtype=jnp.int32)[:, None]
    for layer_index in range(qkv_weight.shape[0]):
        normed = rms_scale(hidden, norm_gain[layer_index]).astype(jnp.bfloat16)
        mixed = jnp.dot(normed.reshape(step_count * row_count, model_width), qkv_weight[layer_index], preferred_element_type=jnp.float32)
        mixed = mixed.reshape(step_count, row_count, groups, per_group, head_dim)
        queries = rotate(rms_scale(mixed[:, :, :, :per_group - 2], query_gain[layer_index]), positions[:, :, None, None]).astype(jnp.bfloat16)
        new_keys = rotate(rms_scale(mixed[:, :, :, per_group - 2], key_gain[layer_index]), positions[:, :, None]).astype(jnp.bfloat16)
        new_values = mixed[:, :, :, per_group - 1].astype(jnp.bfloat16)
        attended = attend(queries, new_keys, new_values, old_keys[layer_index], old_values[layer_index], lengths)
        attended = attended.reshape(step_count * row_count, -1)
        projected = lax.dot_general(attended, out_weight[layer_index], (((1,), (1,)), ((), ())), preferred_element_type=jnp.float32)
        hidden = (hidden.astype(jnp.float32) + projected.reshape(step_count, row_count, model_width)).astype(jnp.bfloat16)
    return hidden

def reference(inputs, qkv_weight, out_weight, norm_gain, query_gain, key_gain, stored_rotated_keys, stored_cache_values, lengths):
    hidden_groups = inputs.reshape(STEPS, N_REP, REPLICA_ROWS, D).transpose(1, 0, 2, 3)
    grouped_keys = jnp.moveaxis(stored_rotated_keys.reshape(LAYER_COUNT, N_REP, REPLICA_ROWS, KEY_VALUE_HEADS, CACHE_SLOTS, HEAD_SIZE), 1, 0)
    grouped_values = jnp.moveaxis(stored_cache_values.reshape(LAYER_COUNT, N_REP, REPLICA_ROWS, KEY_VALUE_HEADS, CACHE_SLOTS, HEAD_SIZE), 1, 0)
    length_groups = lengths.reshape(N_REP, REPLICA_ROWS)

    def one_replica(group):
        return decode_replica(group[0], group[1], group[2], group[3], qkv_weight, out_weight, norm_gain, query_gain, key_gain)
    result = lax.map(one_replica, (hidden_groups, grouped_keys, grouped_values, length_groups))
    return result.transpose(1, 0, 2, 3).reshape(STEPS, REPLICA_ROW_TOTAL, D)
```

```python
import functools

import jax
import jax.numpy as jnp
from jax import lax
from jax.experimental import pallas as pl
from jax.experimental.pallas import tpu as pltpu
from jax.sharding import PartitionSpec as P

epsilon = 1e-06
rope_base = 1000000.0
MIB = 1024 * 1024
VMEM = pltpu.VMEM
SMEM = pltpu.SMEM


def vmem_spec():
    return pl.BlockSpec(memory_space=VMEM)


def smem_spec():
    return pl.BlockSpec(memory_space=SMEM)


def any_spec():
    return pl.BlockSpec(memory_space=pl.ANY)


def tiles(width, size=256):
    return [(start, min(size, width - start)) for start in range(0, width, size)]


def split_kernel(parts, replicas, piece, place_ref, whole_ref, blocks_ref):
    for part in range(parts):
        columns = [
            whole_ref[:, (r * parts + part) * piece : (r * parts + part + 1) * piece]
            for r in range(replicas)
        ]
        blocks_ref[place_ref[part]] = jnp.concatenate(columns, axis=1)


def split_parts(whole, place, parts, replicas, piece):
    rows = whole.shape[0]
    return pl.pallas_call(
        functools.partial(split_kernel, parts, replicas, piece),
        out_shape=jax.ShapeDtypeStruct((parts, rows, replicas * piece), whole.dtype),
        in_specs=[smem_spec(), vmem_spec()],
        out_specs=vmem_spec(),
        compiler_params=pltpu.CompilerParams(vmem_limit_bytes=24 * MIB),
    )(place, whole)


def share_kernel(shares, core_ref, whole_ref, mine_ref, theirs_ref, squares_ref):
    width = mine_ref.shape[1] // shares
    core = core_ref[0]
    squares = None
    for share in range(shares):
        columns = slice(share * width, (share + 1) * width)
        for whose, to_ref in ((core, mine_ref), (1 - core, theirs_ref)):
            start = pl.multiple_of((2 * share + whose) * width, 128)
            some = whole_ref[:, pl.ds(start, width)]
            to_ref[:, columns] = some
            wide = some.astype(jnp.float32)
            term = jnp.sum(wide * wide, axis=1, keepdims=True)
            squares = term if squares is None else squares + term
    squares_ref[...] = squares


def share_features(whole, core, shares):
    rows, width = whole.shape
    part = jax.ShapeDtypeStruct((rows, width // 2), whole.dtype)
    return pl.pallas_call(
        functools.partial(share_kernel, shares),
        out_shape=(part, part, jax.ShapeDtypeStruct((rows, 1), jnp.float32)),
        in_specs=[smem_spec(), vmem_spec()],
        out_specs=(vmem_spec(), vmem_spec(), vmem_spec()),
        compiler_params=pltpu.CompilerParams(vmem_limit_bytes=24 * MIB),
    )(core, whole)


def join_kernel(parts, replicas, piece, place_ref, *refs):
    block_refs, whole_ref, held, sems = refs[:parts], refs[parts], refs[parts + 1], refs[parts + 2]
    copies = [
        pltpu.make_async_copy(block_refs[shift], held.at[place_ref[shift]], sems.at[shift])
        for shift in range(parts)
    ]
    for copy in copies:
        copy.start()
    for copy in copies:
        copy.wait()
    for r in range(replicas):
        columns = [held[part, :, r * piece : (r + 1) * piece] for part in range(parts)]
        whole_ref[:, r * parts * piece : (r + 1) * parts * piece] = jnp.concatenate(columns, axis=1)


def join_parts(blocks, place, replicas, piece):
    parts = len(blocks)
    rows = blocks[0].shape[0]
    return pl.pallas_call(
        functools.partial(join_kernel, parts, replicas, piece),
        out_shape=jax.ShapeDtypeStruct((rows, parts * replicas * piece), blocks[0].dtype),
        in_specs=[smem_spec()] + [any_spec()] * parts,
        out_specs=vmem_spec(),
        scratch_shapes=[
            VMEM((parts, rows, replicas * piece), blocks[0].dtype),
            pltpu.SemaphoreType.DMA((parts,)),
        ],
        compiler_params=pltpu.CompilerParams(vmem_limit_bytes=24 * MIB),
    )(place, *blocks)


def qkv_kernel(count, shifts, pieces, arrays, continued, rows_ref, *refs):
    block_refs, refs = refs[:count], refs[count:]
    gain_ref, scale_ref, refs = refs[0], refs[1], refs[2:]
    weight_refs, refs = refs[:arrays], refs[arrays:]
    outputs = (len(refs) - 3) // (2 if continued else 1)
    if continued:
        before_refs, refs = refs[:outputs], refs[outputs:]
    mixed_refs, refs = refs[:outputs], refs[outputs:]
    held, normed, sems = refs
    each = mixed_refs[0].shape[0]
    copies = []
    for index, (array, first, size, place) in enumerate(pieces):
        to = pl.multiple_of(rows_ref[index], 16)
        copies.append(
            pltpu.make_async_copy(
                weight_refs[array].at[pl.ds(first, size)],
                held.at[place, pl.ds(to, size)],
                sems.at[index],
            )
        )
        copies[-1].start()
    step = 32

    @pl.loop(0, normed.shape[1] // step)
    def _(tile):
        rows = pl.ds(pl.multiple_of(tile * step, step), step)
        scale = scale_ref[rows, :]
        for place, shift in enumerate(shifts):
            wide = block_refs[place][rows, :].astype(jnp.float32)
            normed[place, rows, :] = (wide * scale * gain_ref[shift]).astype(jnp.bfloat16)

    for place in range(count):
        for index in range(len(pieces)):
            if pieces[index][3] == place:
                copies[index].wait()
        for start, size in tiles(mixed_refs[0].shape[1]):
            columns = slice(start, start + size)
            terms = jnp.dot(
                normed[place], held[place, :, columns], preferred_element_type=jnp.float32
            )
            for index in range(outputs):
                term = terms[index * each : (index + 1) * each]
                if place > 0:
                    mixed_refs[index][:, columns] += term
                elif continued:
                    mixed_refs[index][:, columns] = before_refs[index][:, columns] + term
                else:
                    mixed_refs[index][:, columns] = term


def project_qkv(
    blocks, shifts, gains, scale, weights, pieces, rows, before=None, outputs=1
):
    count = len(shifts)
    row_total, width = blocks[0].shape
    columns = weights[0].shape[1]
    continued = before is not None
    operands = [rows] + [blocks[shift] for shift in shifts] + [gains, scale] + list(weights)
    in_specs = [smem_spec()] + [vmem_spec()] * (count + 2) + [any_spec()] * len(weights)
    if continued:
        operands += list(before)
        in_specs += [vmem_spec()] * outputs
    mixed = jax.ShapeDtypeStruct((row_total // outputs, columns), jnp.float32)
    return pl.pallas_call(
        functools.partial(qkv_kernel, count, shifts, pieces, len(weights), continued),
        out_shape=[mixed] * outputs,
        in_specs=in_specs,
        out_specs=[vmem_spec()] * outputs,
        scratch_shapes=[
            VMEM((count, width, columns), jnp.bfloat16),
            VMEM((count, row_total, width), jnp.bfloat16),
            pltpu.SemaphoreType.DMA((len(pieces),)),
        ],
        compiler_params=pltpu.CompilerParams(vmem_limit_bytes=52 * MIB),
        cost_estimate=pl.CostEstimate(
            flops=2 * row_total * count * width * columns,
            bytes_accessed=2 * count * width * columns,
            transcendentals=0,
        ),
    )(*operands)


def whole_out_kernel(count, column_ref, *refs):
    attended_refs, refs = refs[:count], refs[count:]
    weight_ref, residual_ref, hidden_ref, held, total, sems = refs
    width = attended_refs[0].shape[1]
    copies = []
    for shift in range(count):
        start = pl.multiple_of(column_ref[shift], 128)
        copies.append(
            pltpu.make_async_copy(
                weight_ref.at[:, pl.ds(start, width)], held.at[shift], sems.at[shift]
            )
        )
        copies[-1].start()
    for shift in range(count):
        copies[shift].wait()
        for start, size in tiles(hidden_ref.shape[1]):
            features = slice(start, start + size)
            term = lax.dot_general(
                attended_refs[shift][...],
                held[shift, features, :],
                (((1,), (1,)), ((), ())),
                preferred_element_type=jnp.float32,
            )
            if shift > 0:
                term = total[:, features] + term
            if shift < count - 1:
                total[:, features] = term
            else:
                hidden_ref[:, features] = (
                    residual_ref[:, features].astype(jnp.float32) + term
                ).astype(hidden_ref.dtype)


def project_out_whole(attended, weight, columns, residual):
    count = len(attended)
    row_total, width = attended[0].shape
    features = weight.shape[0]
    return pl.pallas_call(
        functools.partial(whole_out_kernel, count),
        out_shape=jax.ShapeDtypeStruct((row_total, features), residual.dtype),
        in_specs=[smem_spec()] + [vmem_spec()] * count + [any_spec(), vmem_spec()],
        out_specs=vmem_spec(),
        scratch_shapes=[
            VMEM((count, features, width), jnp.bfloat16),
            VMEM((row_total, features), jnp.float32),
            pltpu.SemaphoreType.DMA((count,)),
        ],
        compiler_params=pltpu.CompilerParams(vmem_limit_bytes=50 * MIB),
        cost_estimate=pl.CostEstimate(
            flops=2 * row_total * count * width * features,
            bytes_accessed=2 * count * width * features,
            transcendentals=0,
        ),
    )(columns, *attended, weight, residual)


def out_kernel(count, shifts, column_ref, *refs):
    attended_refs, refs = refs[:count], refs[count:]
    weight_ref, refs = refs[0], refs[1:]
    last = len(refs) > 3
    if last:
        before_ref, residual_ref, refs = refs[0], refs[1], refs[2:]
    sum_ref, held, sems = refs[0], refs[-2], refs[-1]
    width = attended_refs[0].shape[1]
    copies = []
    for place, shift in enumerate(shifts):
        start = pl.multiple_of(column_ref[shift], 128)
        copies.append(
            pltpu.make_async_copy(
                weight_ref.at[:, pl.ds(start, width)], held.at[place], sems.at[place]
            )
        )
        copies[-1].start()
    for place in range(count):
        copies[place].wait()
        for start, size in tiles(sum_ref.shape[1]):
            features = slice(start, start + size)
            term = lax.dot_general(
                attended_refs[place][...],
                held[place, features, :],
                (((1,), (1,)), ((), ())),
                preferred_element_type=jnp.float32,
            )
            if last:
                total = before_ref[:, features] + term
                total = residual_ref[:, features].astype(jnp.float32) + total
                sum_ref[:, features] = total.astype(sum_ref.dtype)
            elif place > 0:
                sum_ref[:, features] += term
            else:
                sum_ref[:, features] = term


def project_out(attended, shifts, weight, columns, before=None, residual=None):
    count = len(shifts)
    row_total, width = attended[0].shape
    features = weight.shape[0]
    last = residual is not None
    operands = [columns] + [attended[shift] for shift in shifts] + [weight]
    in_specs = [smem_spec()] + [vmem_spec()] * count + [any_spec()]
    if last:
        operands += [before, residual]
        in_specs += [vmem_spec()] * 2
    return pl.pallas_call(
        functools.partial(out_kernel, count, shifts),
        out_shape=jax.ShapeDtypeStruct(
            (row_total, features), residual.dtype if last else jnp.float32
        ),
        in_specs=in_specs,
        out_specs=vmem_spec(),
        scratch_shapes=[
            VMEM((count, features, width), jnp.bfloat16),
            pltpu.SemaphoreType.DMA((count,)),
        ],
        compiler_params=pltpu.CompilerParams(vmem_limit_bytes=50 * MIB),
        cost_estimate=pl.CostEstimate(
            flops=2 * row_total * count * width * features,
            bytes_accessed=2 * count * width * features,
            transcendentals=0,
        ),
    )(*operands)


def attention_kernel(heads, lengths_ref, *refs):
    mixed_refs, refs = refs[:-9], refs[-9:]
    cosine_ref, sine_ref, query_gain_ref, key_gain_ref, keys_ref, values_ref = refs[:6]
    attended_ref, query_rows, result_rows = refs[6:]
    steps, rows, _ = mixed_refs[0].shape
    slots, size = keys_ref.shape[-2:]
    step_rows = steps * rows
    per_row = heads * steps
    first_row = pl.program_id(0) * rows
    scale = size ** (-0.5)
    cosine = cosine_ref[...]
    sine = sine_ref[...]

    def projected(vector):
        columns = slice(vector * size, (vector + 1) * size)
        return sum(ref[:, :, columns] for ref in mixed_refs)

    def turned(vectors, gain):
        mean = jnp.mean(vectors * vectors, axis=-1, keepdims=True)
        normal = vectors * lax.rsqrt(mean + epsilon) * gain
        swapped = jnp.concatenate([normal[..., size // 2 :], normal[..., : size // 2]], axis=-1)
        return normal * cosine + swapped * sine

    for head in range(heads):
        vectors = projected(head)
        query = turned(vectors, query_gain_ref[...])
        query_rows[head * step_rows : (head + 1) * step_rows, :] = query.reshape(step_rows, size)
    new_key = turned(projected(heads), key_gain_ref[...])
    new_key = new_key.reshape(step_rows, size).astype(jnp.bfloat16)
    new_value = projected(heads + 1)
    new_value = new_value.reshape(step_rows, size).astype(jnp.bfloat16)

    queries = [
        query_rows[pl.ds(r, per_row, stride=rows), :].astype(jnp.bfloat16) for r in range(rows)
    ]
    nt = (((1,), (1,)), ((), ()))
    column = lax.broadcasted_iota(jnp.int32, (per_row, slots), 1)
    old = []
    for r in range(rows):
        score = lax.dot_general(
            queries[r], keys_ref[r], nt, preferred_element_type=jnp.float32
        )
        old.append(jnp.where(column < lengths_ref[first_row + r], score * scale, -jnp.inf))
    old = jnp.concatenate(old, axis=0)
    new = lax.dot_general(
        jnp.concatenate(queries, axis=0), new_key, nt, preferred_element_type=jnp.float32
    )
    at = lax.broadcasted_iota(jnp.int32, (rows * per_row, step_rows), 0)
    to = lax.broadcasted_iota(jnp.int32, (rows * per_row, step_rows), 1)
    seen = (at // per_row == to % rows) & (to // rows <= at % steps)
    new = jnp.where(seen, new * scale, -jnp.inf)
    highest = jnp.maximum(
        jnp.max(old, axis=-1, keepdims=True), jnp.max(new, axis=-1, keepdims=True)
    )
    old = jnp.exp(old - highest)
    new = jnp.exp(new - highest)
    total = jnp.sum(old, axis=-1, keepdims=True) + jnp.sum(new, axis=-1, keepdims=True)
    old = (old / total).astype(jnp.bfloat16)
    new = (new / total).astype(jnp.bfloat16)
    from_new = jnp.dot(new, new_value, preferred_element_type=jnp.float32)
    for r in range(rows):
        part = slice(r * per_row, (r + 1) * per_row)
        result = jnp.dot(old[part], values_ref[r], preferred_element_type=jnp.float32)
        result_rows[pl.ds(r, per_row, stride=rows), :] = result + from_new[part]
    for head in range(heads):
        result = result_rows[head * step_rows : (head + 1) * step_rows, :]
        attended_ref[:, :, head * size : (head + 1) * size] = result.reshape(
            steps, rows, size
        ).astype(jnp.bfloat16)


def attend(mixed, cosine, sine, query_gain, key_gain, keys, values, lengths, layer):
    steps, row_total, columns = mixed[0].shape
    groups, slots, size = keys.shape[2:]
    per_group = columns // (groups * size)
    heads = per_group - 2
    rows = 16
    cache_spec = pl.BlockSpec(
        (None, rows, None, slots, size), lambda i, g, _: (layer, i, g, 0, 0)
    )
    turn_spec = pl.BlockSpec((steps, rows, size), lambda i, g, _: (0, i, 0))
    gain_spec = pl.BlockSpec((1, size), lambda i, g, _: (0, 0))
    return pl.pallas_call(
        functools.partial(attention_kernel, heads),
        out_shape=jax.ShapeDtypeStruct((steps, row_total, groups * heads * size), jnp.bfloat16),
        grid_spec=pltpu.PrefetchScalarGridSpec(
            num_scalar_prefetch=1,
            grid=(row_total // rows, groups),
            in_specs=[pl.BlockSpec((steps, rows, per_group * size), lambda i, g, _: (0, i, g))]
            * len(mixed)
            + [
                turn_spec,
                turn_spec,
                gain_spec,
                gain_spec,
                cache_spec,
                cache_spec,
            ],
            out_specs=pl.BlockSpec((steps, rows, heads * size), lambda i, g, _: (0, i, g)),
            scratch_shapes=[
                VMEM((heads * steps * rows, size), jnp.float32),
                VMEM((heads * steps * rows, size), jnp.float32),
            ],
        ),
        compiler_params=pltpu.CompilerParams(vmem_limit_bytes=49 * MIB),
        cost_estimate=pl.CostEstimate(
            flops=4 * row_total * groups * heads * steps * slots * size,
            bytes_accessed=4 * row_total * groups * slots * size,
            transcendentals=row_total * groups * heads * steps * slots,
        ),
    )(lengths, *mixed, cosine, sine, query_gain, key_gain, keys, values)


def on_device(
    inputs,
    qkv_weight,
    out_weight,
    norm_gain,
    query_gain,
    key_gain,
    stored_rotated_keys,
    stored_cache_values,
    lengths,
):
    step_count, row_count, model_width = inputs.shape
    flat_rows = step_count * row_count
    layers = qkv_weight.shape[0]
    head_dim = stored_rotated_keys.shape[4]
    parts = lax.axis_size("tp")
    replicas = lax.axis_size("rep")
    me = lax.axis_index("tp")
    piece = qkv_weight.shape[1]
    slice_width = replicas * piece
    block_width = qkv_weight.shape[2] // parts
    head_width = out_weight.shape[2] // parts
    merge = piece % 16 == 0

    def shifted(block, shift):
        if shift == 0:
            return block
        return lax.ppermute(block, "tp", [(i, (i + shift) % parts) for i in range(parts)])

    def all_parts(block, *earlier):
        if parts != 4:
            return [shifted(block, shift) for shift in range(parts)]
        one, three = shifted(block, 1), shifted(block, 3)
        from_left, from_right = one, three
        if earlier:
            from_left, from_right = lax.optimization_barrier((one, three) + earlier)[:2]
        rightwards = lax.ppermute(from_left, "tp", [(1, 2), (2, 3)])
        leftwards = lax.ppermute(from_right, "tp", [(1, 0), (2, 1)])
        return [block, one, jnp.where(me >= 2, rightwards, leftwards), three]

    def outgoing(layer, shift):
        target = lax.rem(me + shift, parts)
        return lax.dynamic_slice(
            qkv_weight, (layer, 0, target * block_width), (1, piece, block_width)
        )[0]

    source = lax.rem(me - jnp.arange(parts, dtype=jnp.int32) + parts, parts)
    seat = lax.axis_index("rep")
    by_links = merge and replicas == 8 and parts == 4 and layers == 2

    def after(array, *earlier):
        return lax.optimization_barrier((array,) + earlier)[0]

    def swapped(block, mask):
        return lax.ppermute(block, "rep", [(i, i ^ mask) for i in range(replicas)])

    def spread_first(block, *earlier):
        block = after(block, *earlier) if earlier else block
        return [(0, 0, block), (2, 0, swapped(block, 2)), (4, 0, swapped(block, 4))]

    def spread_second(spread):
        by_x, by_y = spread[1][2], spread[2][2]
        half = by_x.shape[0] // 2
        return spread + [(6, 0, swapped(by_x[:half], 4)), (6, half, swapped(by_y[half:], 2))]

    def listed(spreads, shifts):
        arrays, pieces, rows = [], [], []
        for spread, its_shifts in zip(spreads, shifts):
            for mask, first, array in spread:
                at = 0
                while at < array.shape[0]:
                    place, offset = divmod(first + at, piece)
                    count = min(piece - offset, array.shape[0] - at)
                    pieces.append((len(arrays), at, count, its_shifts[place]))
                    rows.append(((seat ^ mask) // 2) * piece + offset)
                    at += count
                arrays.append(array)
        return arrays, pieces, jnp.stack(rows).astype(jnp.int32)

    positions = lengths[None, :] + jnp.arange(step_count, dtype=jnp.int32)[:, None]
    half = head_dim // 2
    frequency = rope_base ** (-jnp.arange(half, dtype=jnp.float32) / half)
    angles = positions.astype(jnp.float32)[..., None] * frequency
    cosine, sine = jnp.cos(angles), jnp.sin(angles)
    cosine = jnp.concatenate([cosine, cosine], axis=-1)
    sine = jnp.concatenate([-sine, sine], axis=-1)

    gains = jnp.take(norm_gain.reshape(layers, replicas, parts, piece), source, axis=2)
    gains = jnp.moveaxis(gains, 2, 1).reshape(layers, parts, 1, slice_width)

    flat = inputs.reshape(flat_rows, model_width)
    blocks = split_parts(flat, source, parts, replicas, piece)
    hidden = [blocks[shift] for shift in range(parts)]

    def from_calls(layer):
        arrays = [
            lax.all_gather(shifted(outgoing(layer, shift), shift), "rep", axis=0, tiled=True)
            for shift in range(parts)
        ]
        pieces = [(shift, 0, slice_width, shift) for shift in range(parts)]
        return arrays, pieces, jnp.zeros((parts,), jnp.int32)

    def from_call(came):
        array = lax.all_gather(came, "rep", axis=0, tiled=True)
        pieces = [
            (0, (r * parts + shift) * piece, piece, shift)
            for r in range(replicas)
            for shift in range(parts)
        ]
        rows = jnp.array([r * piece for r in range(replicas) for _ in range(parts)], jnp.int32)
        return [array], pieces, rows

    stages = [[0, 1, 3], [2]]

    def row_scale(squares):
        return lax.rsqrt(squares / model_width + epsilon)

    if by_links:
        core = lax.rem(seat, 2)
        mine, theirs, squares = share_features(
            flat, jnp.full((1,), core, jnp.int32), replicas // 2
        )
        both = jnp.concatenate([mine, swapped(theirs, 1)], axis=0)
        both = split_parts(both, source, parts, replicas // 2, piece)
        both = [both[shift] for shift in range(parts)]
        other = swapped(squares.reshape(-1, 128), 1).reshape(flat_rows, 1)
        scale = row_scale(jnp.concatenate([squares, other], axis=0))
        core_gains = lax.dynamic_index_in_dim(
            gains[0].reshape(parts, replicas // 2, 2, piece), core, 2, keepdims=False
        ).reshape(parts, 1, slice_width // 2)
        one, three = shifted(outgoing(0, 1), 1), shifted(outgoing(0, 3), 3)
        two = shifted(after(outgoing(0, 2), one, three), 2)
        head = spread_first(outgoing(0, 0))
        body = spread_first(
            jnp.concatenate([one, three], axis=0), head[1][2], head[2][2]
        )
        head = spread_second(head)
        turned = [array for _, _, array in head[3:5]]
        tail = spread_first(two, body[1][2], body[2][2], *turned)
        ahead = [array for _, _, array in body[1:3]]
        across = [array for _, _, array in tail[1:3]]
        body = spread_second(body)
        tail = spread_second(tail)
        gathers = [[listed([head, body], [[0], [1, 2]]), listed([tail], [[0]])]]
        later_one = shifted(after(outgoing(1, 1), two), 1)
        later_two = shifted(after(outgoing(1, 2), across[0], across[1]), 2)
        later_three = shifted(after(outgoing(1, 3), later_two), 3)
        came = (outgoing(1, 0), later_one, later_two, later_three)
        sent = [after(out_weight[0], *ahead, *turned, two, scale, *both), out_weight[1]]
    else:
        wide = flat.astype(jnp.float32)
        squares = jnp.sum(wide * wide, axis=1, keepdims=True)
        gathers = [from_calls(layer) for layer in range(layers)]
        sent = [out_weight[layer] for layer in range(layers)]
    outs = [lax.all_gather(one, "rep", axis=0, tiled=True) for one in sent]

    columns = source * head_width
    for layer in range(layers):
        if by_links and layer == 0:
            mixed = None
            for stage, (arrays, pieces, rows) in zip(stages, gathers[0]):
                if mixed is not None:
                    mixed = lax.optimization_barrier(
                        (*mixed, later_one, later_two)
                    )[:2]
                mixed = project_qkv(
                    both, stage, core_gains, scale, arrays, pieces, rows, mixed, outputs=2
                )
            mixed = [mixed[0], swapped(mixed[1], 1)]
        else:
            mixed = project_qkv(
                hidden, list(range(parts)), gains[layer], row_scale(squares), *gathers[layer]
            )
        attended = attend(
            [one.reshape(step_count, row_count, block_width) for one in mixed],
            cosine,
            sine,
            query_gain[layer][None],
            key_gain[layer][None],
            stored_rotated_keys,
            stored_cache_values,
            lengths,
            layer,
        ).reshape(flat_rows, head_width)
        if by_links and layer + 1 < layers:
            came = lax.optimization_barrier(came + (attended,))[:parts]
            gathers.append(from_call(jnp.concatenate(came, axis=0)))
        if by_links and layer == 0:
            attended = all_parts(attended, outs[layer])
            own = project_out(attended, stages[0], outs[layer], columns)
            own = project_out(attended, stages[1], outs[layer], columns, own, hidden[0])
        else:
            own = project_out_whole(all_parts(attended), outs[layer], columns, hidden[0])
        if layer + 1 < layers:
            wide = own.astype(jnp.float32)
            mine = jnp.sum(wide * wide, axis=1).reshape(-1, 128)
            squares = sum(shifted(mine, shift) for shift in range(parts))
            hidden = all_parts(own, squares)
            squares = squares.reshape(flat_rows, 1)
        else:
            hidden = all_parts(own)
    joined = join_parts(hidden, source, replicas, piece)
    return joined.reshape(step_count, row_count, model_width)


def solution(mesh):
    return jax.shard_map(
        on_device,
        mesh=mesh,
        in_specs=(
            P(None, "rep", None),
            P(None, ("rep", "tp"), None),
            P(None, ("rep", "tp"), None),
            P(),
            P(),
            P(),
            P(None, "rep", "tp", None, None),
            P(None, "rep", "tp", None, None),
            P("rep"),
        ),
        out_specs=P(None, "rep", None),
        check_vma=False,
    )
```

```python
import functools

import jax
import jax.numpy as jnp
from jax import lax
from jax.experimental import pallas as pl
from jax.experimental.pallas import tpu as pltpu
from jax.sharding import PartitionSpec as P

epsilon = 1e-06
rope_base = 1000000.0
MIB = 1024 * 1024
VMEM = pltpu.VMEM
SMEM = pltpu.SMEM


def vmem_spec():
    return pl.BlockSpec(memory_space=VMEM)


def smem_spec():
    return pl.BlockSpec(memory_space=SMEM)


def any_spec():
    return pl.BlockSpec(memory_space=pl.ANY)


def tiles(width, size=256):
    return [(start, min(size, width - start)) for start in range(0, width, size)]


def split_kernel(parts, replicas, piece, place_ref, whole_ref, blocks_ref):
    for part in range(parts):
        columns = [
            whole_ref[:, (r * parts + part) * piece : (r * parts + part + 1) * piece]
            for r in range(replicas)
        ]
        blocks_ref[place_ref[part]] = jnp.concatenate(columns, axis=1)


def split_parts(whole, place, parts, replicas, piece):
    rows = whole.shape[0]
    return pl.pallas_call(
        functools.partial(split_kernel, parts, replicas, piece),
        out_shape=jax.ShapeDtypeStruct((parts, rows, replicas * piece), whole.dtype),
        in_specs=[smem_spec(), vmem_spec()],
        out_specs=vmem_spec(),
        compiler_params=pltpu.CompilerParams(vmem_limit_bytes=24 * MIB),
    )(place, whole)


def share_kernel(shares, core_ref, whole_ref, mine_ref, theirs_ref, squares_ref):
    width = mine_ref.shape[1] // shares
    core = core_ref[0]
    squares = None
    for share in range(shares):
        columns = slice(share * width, (share + 1) * width)
        for whose, to_ref in ((core, mine_ref), (1 - core, theirs_ref)):
            start = pl.multiple_of((2 * share + whose) * width, 128)
            some = whole_ref[:, pl.ds(start, width)]
            to_ref[:, columns] = some
            wide = some.astype(jnp.float32)
            term = jnp.sum(wide * wide, axis=1, keepdims=True)
            squares = term if squares is None else squares + term
    squares_ref[...] = squares


def share_features(whole, core, shares):
    rows, width = whole.shape
    part = jax.ShapeDtypeStruct((rows, width // 2), whole.dtype)
    return pl.pallas_call(
        functools.partial(share_kernel, shares),
        out_shape=(part, part, jax.ShapeDtypeStruct((rows, 1), jnp.float32)),
        in_specs=[smem_spec(), vmem_spec()],
        out_specs=(vmem_spec(), vmem_spec(), vmem_spec()),
        compiler_params=pltpu.CompilerParams(vmem_limit_bytes=24 * MIB),
    )(core, whole)


def join_kernel(parts, replicas, piece, place_ref, *refs):
    block_refs, whole_ref, held, sems = refs[:parts], refs[parts], refs[parts + 1], refs[parts + 2]
    copies = [
        pltpu.make_async_copy(block_refs[shift], held.at[place_ref[shift]], sems.at[shift])
        for shift in range(parts)
    ]
    for copy in copies:
        copy.start()
    for copy in copies:
        copy.wait()
    for r in range(replicas):
        columns = [held[part, :, r * piece : (r + 1) * piece] for part in range(parts)]
        whole_ref[:, r * parts * piece : (r + 1) * parts * piece] = jnp.concatenate(columns, axis=1)


def join_parts(blocks, place, replicas, piece):
    parts = len(blocks)
    rows = blocks[0].shape[0]
    return pl.pallas_call(
        functools.partial(join_kernel, parts, replicas, piece),
        out_shape=jax.ShapeDtypeStruct((rows, parts * replicas * piece), blocks[0].dtype),
        in_specs=[smem_spec()] + [any_spec()] * parts,
        out_specs=vmem_spec(),
        scratch_shapes=[
            VMEM((parts, rows, replicas * piece), blocks[0].dtype),
            pltpu.SemaphoreType.DMA((parts,)),
        ],
        compiler_params=pltpu.CompilerParams(vmem_limit_bytes=24 * MIB),
    )(place, *blocks)


def qkv_kernel(count, shifts, pieces, arrays, scaled, continued, rows_ref, *refs):
    block_refs, refs = refs[:count], refs[count:]
    gain_ref, refs = refs[0], refs[1:]
    if scaled:
        scale_ref, refs = refs[0], refs[1:]
    weight_refs, refs = refs[:arrays], refs[arrays:]
    outputs = (len(refs) - 3) // (2 if continued else 1)
    if continued:
        before_refs, refs = refs[:outputs], refs[outputs:]
    mixed_refs, refs = refs[:outputs], refs[outputs:]
    held, normed, sems = refs
    each = mixed_refs[0].shape[0]
    copies = []
    for index, (array, first, size, place) in enumerate(pieces):
        to = pl.multiple_of(rows_ref[index], 16)
        copies.append(
            pltpu.make_async_copy(
                weight_refs[array].at[pl.ds(first, size)],
                held.at[place, pl.ds(to, size)],
                sems.at[index],
            )
        )
        copies[-1].start()
    step = 32

    @pl.loop(0, normed.shape[1] // step)
    def _(tile):
        rows = pl.ds(pl.multiple_of(tile * step, step), step)
        if scaled:
            scale = scale_ref[rows, :]
        else:
            squares = None
            for ref in block_refs:
                wide = ref[rows, :].astype(jnp.float32)
                term = jnp.sum(wide * wide, axis=-1, keepdims=True)
                squares = term if squares is None else squares + term
            scale = lax.rsqrt(squares / (count * normed.shape[2]) + epsilon)
        for place, shift in enumerate(shifts):
            wide = block_refs[place][rows, :].astype(jnp.float32)
            normed[place, rows, :] = (wide * scale * gain_ref[shift]).astype(jnp.bfloat16)

    for place in range(count):
        for index in range(len(pieces)):
            if pieces[index][3] == place:
                copies[index].wait()
        for start, size in tiles(mixed_refs[0].shape[1]):
            columns = slice(start, start + size)
            terms = jnp.dot(
                normed[place], held[place, :, columns], preferred_element_type=jnp.float32
            )
            for index in range(outputs):
                term = terms[index * each : (index + 1) * each]
                if place > 0:
                    mixed_refs[index][:, columns] += term
                elif continued:
                    mixed_refs[index][:, columns] = before_refs[index][:, columns] + term
                else:
                    mixed_refs[index][:, columns] = term


def project_qkv(
    blocks, shifts, gains, scale, weights, pieces, rows, before=None, outputs=1
):
    count = len(shifts)
    row_total, width = blocks[0].shape
    columns = weights[0].shape[1]
    continued = before is not None
    scaled = scale is not None
    operands = [rows] + [blocks[shift] for shift in shifts] + [gains] + [scale] * scaled
    in_specs = [smem_spec()] + [vmem_spec()] * (len(operands) - 1) + [any_spec()] * len(weights)
    operands += list(weights)
    if continued:
        operands += list(before)
        in_specs += [vmem_spec()] * outputs
    mixed = jax.ShapeDtypeStruct((row_total // outputs, columns), jnp.float32)
    return pl.pallas_call(
        functools.partial(
            qkv_kernel, count, shifts, pieces, len(weights), scaled, continued
        ),
        out_shape=[mixed] * outputs,
        in_specs=in_specs,
        out_specs=[vmem_spec()] * outputs,
        scratch_shapes=[
            VMEM((count, width, columns), jnp.bfloat16),
            VMEM((count, row_total, width), jnp.bfloat16),
            pltpu.SemaphoreType.DMA((len(pieces),)),
        ],
        compiler_params=pltpu.CompilerParams(vmem_limit_bytes=(52 if scaled else 40) * MIB),
        cost_estimate=pl.CostEstimate(
            flops=2 * row_total * count * width * columns,
            bytes_accessed=2 * count * width * columns,
            transcendentals=0,
        ),
    )(*operands)


def whole_out_kernel(count, column_ref, *refs):
    attended_refs, refs = refs[:count], refs[count:]
    weight_ref, residual_ref, hidden_ref, held, total, sems = refs
    width = attended_refs[0].shape[1]
    copies = []
    for shift in range(count):
        start = pl.multiple_of(column_ref[shift], 128)
        copies.append(
            pltpu.make_async_copy(
                weight_ref.at[:, pl.ds(start, width)], held.at[shift], sems.at[shift]
            )
        )
        copies[-1].start()
    for shift in range(count):
        copies[shift].wait()
        for start, size in tiles(hidden_ref.shape[1]):
            features = slice(start, start + size)
            term = lax.dot_general(
                attended_refs[shift][...],
                held[shift, features, :],
                (((1,), (1,)), ((), ())),
                preferred_element_type=jnp.float32,
            )
            if shift > 0:
                term = total[:, features] + term
            if shift < count - 1:
                total[:, features] = term
            else:
                hidden_ref[:, features] = (
                    residual_ref[:, features].astype(jnp.float32) + term
                ).astype(hidden_ref.dtype)


def project_out_whole(attended, weight, columns, residual):
    count = len(attended)
    row_total, width = attended[0].shape
    features = weight.shape[0]
    return pl.pallas_call(
        functools.partial(whole_out_kernel, count),
        out_shape=jax.ShapeDtypeStruct((row_total, features), residual.dtype),
        in_specs=[smem_spec()] + [vmem_spec()] * count + [any_spec(), vmem_spec()],
        out_specs=vmem_spec(),
        scratch_shapes=[
            VMEM((count, features, width), jnp.bfloat16),
            VMEM((row_total, features), jnp.float32),
            pltpu.SemaphoreType.DMA((count,)),
        ],
        compiler_params=pltpu.CompilerParams(vmem_limit_bytes=50 * MIB),
        cost_estimate=pl.CostEstimate(
            flops=2 * row_total * count * width * features,
            bytes_accessed=2 * count * width * features,
            transcendentals=0,
        ),
    )(columns, *attended, weight, residual)


def out_kernel(count, shifts, column_ref, *refs):
    attended_refs, refs = refs[:count], refs[count:]
    weight_ref, refs = refs[0], refs[1:]
    last = len(refs) > 3
    if last:
        before_ref, residual_ref, refs = refs[0], refs[1], refs[2:]
    sum_ref, held, sems = refs[0], refs[-2], refs[-1]
    width = attended_refs[0].shape[1]
    copies = []
    for place, shift in enumerate(shifts):
        start = pl.multiple_of(column_ref[shift], 128)
        copies.append(
            pltpu.make_async_copy(
                weight_ref.at[:, pl.ds(start, width)], held.at[place], sems.at[place]
            )
        )
        copies[-1].start()
    for place in range(count):
        copies[place].wait()
        for start, size in tiles(sum_ref.shape[1]):
            features = slice(start, start + size)
            term = lax.dot_general(
                attended_refs[place][...],
                held[place, features, :],
                (((1,), (1,)), ((), ())),
                preferred_element_type=jnp.float32,
            )
            if last:
                total = before_ref[:, features] + term
                total = residual_ref[:, features].astype(jnp.float32) + total
                sum_ref[:, features] = total.astype(sum_ref.dtype)
            elif place > 0:
                sum_ref[:, features] += term
            else:
                sum_ref[:, features] = term


def project_out(attended, shifts, weight, columns, before=None, residual=None):
    count = len(shifts)
    row_total, width = attended[0].shape
    features = weight.shape[0]
    last = residual is not None
    operands = [columns] + [attended[shift] for shift in shifts] + [weight]
    in_specs = [smem_spec()] + [vmem_spec()] * count + [any_spec()]
    if last:
        operands += [before, residual]
        in_specs += [vmem_spec()] * 2
    return pl.pallas_call(
        functools.partial(out_kernel, count, shifts),
        out_shape=jax.ShapeDtypeStruct(
            (row_total, features), residual.dtype if last else jnp.float32
        ),
        in_specs=in_specs,
        out_specs=vmem_spec(),
        scratch_shapes=[
            VMEM((count, features, width), jnp.bfloat16),
            pltpu.SemaphoreType.DMA((count,)),
        ],
        compiler_params=pltpu.CompilerParams(vmem_limit_bytes=50 * MIB),
        cost_estimate=pl.CostEstimate(
            flops=2 * row_total * count * width * features,
            bytes_accessed=2 * count * width * features,
            transcendentals=0,
        ),
    )(*operands)


def attention_kernel(heads, lengths_ref, *refs):
    mixed_refs, refs = refs[:-9], refs[-9:]
    cosine_ref, sine_ref, query_gain_ref, key_gain_ref, keys_ref, values_ref = refs[:6]
    attended_ref, query_rows, result_rows = refs[6:]
    steps, rows, _ = mixed_refs[0].shape
    slots, size = keys_ref.shape[-2:]
    step_rows = steps * rows
    per_row = heads * steps
    first_row = pl.program_id(0) * rows
    scale = size ** (-0.5)
    cosine = cosine_ref[...]
    sine = sine_ref[...]

    def projected(vector):
        columns = slice(vector * size, (vector + 1) * size)
        return sum(ref[:, :, columns] for ref in mixed_refs)

    def turned(vectors, gain):
        mean = jnp.mean(vectors * vectors, axis=-1, keepdims=True)
        normal = vectors * lax.rsqrt(mean + epsilon) * gain
        swapped = jnp.concatenate([normal[..., size // 2 :], normal[..., : size // 2]], axis=-1)
        return normal * cosine + swapped * sine

    for head in range(heads):
        vectors = projected(head)
        query = turned(vectors, query_gain_ref[...])
        query_rows[head * step_rows : (head + 1) * step_rows, :] = query.reshape(step_rows, size)
    new_key = turned(projected(heads), key_gain_ref[...])
    new_key = new_key.reshape(step_rows, size).astype(jnp.bfloat16)
    new_value = projected(heads + 1)
    new_value = new_value.reshape(step_rows, size).astype(jnp.bfloat16)

    queries = [
        query_rows[pl.ds(r, per_row, stride=rows), :].astype(jnp.bfloat16) for r in range(rows)
    ]
    nt = (((1,), (1,)), ((), ()))
    column = lax.broadcasted_iota(jnp.int32, (per_row, slots), 1)
    old = []
    for r in range(rows):
        score = lax.dot_general(
            queries[r], keys_ref[r], nt, preferred_element_type=jnp.float32
        )
        old.append(jnp.where(column < lengths_ref[first_row + r], score * scale, -jnp.inf))
    old = jnp.concatenate(old, axis=0)
    new = lax.dot_general(
        jnp.concatenate(queries, axis=0), new_key, nt, preferred_element_type=jnp.float32
    )
    at = lax.broadcasted_iota(jnp.int32, (rows * per_row, step_rows), 0)
    to = lax.broadcasted_iota(jnp.int32, (rows * per_row, step_rows), 1)
    seen = (at // per_row == to % rows) & (to // rows <= at % steps)
    new = jnp.where(seen, new * scale, -jnp.inf)
    highest = jnp.maximum(
        jnp.max(old, axis=-1, keepdims=True), jnp.max(new, axis=-1, keepdims=True)
    )
    old = jnp.exp(old - highest)
    new = jnp.exp(new - highest)
    total = jnp.sum(old, axis=-1, keepdims=True) + jnp.sum(new, axis=-1, keepdims=True)
    old = (old / total).astype(jnp.bfloat16)
    new = (new / total).astype(jnp.bfloat16)
    from_new = jnp.dot(new, new_value, preferred_element_type=jnp.float32)
    for r in range(rows):
        part = slice(r * per_row, (r + 1) * per_row)
        result = jnp.dot(old[part], values_ref[r], preferred_element_type=jnp.float32)
        result_rows[pl.ds(r, per_row, stride=rows), :] = result + from_new[part]
    for head in range(heads):
        result = result_rows[head * step_rows : (head + 1) * step_rows, :]
        attended_ref[:, :, head * size : (head + 1) * size] = result.reshape(
            steps, rows, size
        ).astype(jnp.bfloat16)


def attend(mixed, cosine, sine, query_gain, key_gain, keys, values, lengths, layer):
    steps, row_total, columns = mixed[0].shape
    groups, slots, size = keys.shape[2:]
    per_group = columns // (groups * size)
    heads = per_group - 2
    rows = 16
    cache_spec = pl.BlockSpec(
        (None, rows, None, slots, size), lambda i, g, _: (layer, i, g, 0, 0)
    )
    turn_spec = pl.BlockSpec((steps, rows, size), lambda i, g, _: (0, i, 0))
    gain_spec = pl.BlockSpec((1, size), lambda i, g, _: (0, 0))
    return pl.pallas_call(
        functools.partial(attention_kernel, heads),
        out_shape=jax.ShapeDtypeStruct((steps, row_total, groups * heads * size), jnp.bfloat16),
        grid_spec=pltpu.PrefetchScalarGridSpec(
            num_scalar_prefetch=1,
            grid=(row_total // rows, groups),
            in_specs=[pl.BlockSpec((steps, rows, per_group * size), lambda i, g, _: (0, i, g))]
            * len(mixed)
            + [
                turn_spec,
                turn_spec,
                gain_spec,
                gain_spec,
                cache_spec,
                cache_spec,
            ],
            out_specs=pl.BlockSpec((steps, rows, heads * size), lambda i, g, _: (0, i, g)),
            scratch_shapes=[
                VMEM((heads * steps * rows, size), jnp.float32),
                VMEM((heads * steps * rows, size), jnp.float32),
            ],
        ),
        compiler_params=pltpu.CompilerParams(vmem_limit_bytes=49 * MIB),
        cost_estimate=pl.CostEstimate(
            flops=4 * row_total * groups * heads * steps * slots * size,
            bytes_accessed=4 * row_total * groups * slots * size,
            transcendentals=row_total * groups * heads * steps * slots,
        ),
    )(lengths, *mixed, cosine, sine, query_gain, key_gain, keys, values)


def on_device(
    inputs,
    qkv_weight,
    out_weight,
    norm_gain,
    query_gain,
    key_gain,
    stored_rotated_keys,
    stored_cache_values,
    lengths,
):
    step_count, row_count, model_width = inputs.shape
    flat_rows = step_count * row_count
    layers = qkv_weight.shape[0]
    head_dim = stored_rotated_keys.shape[4]
    parts = lax.axis_size("tp")
    replicas = lax.axis_size("rep")
    me = lax.axis_index("tp")
    piece = qkv_weight.shape[1]
    slice_width = replicas * piece
    block_width = qkv_weight.shape[2] // parts
    head_width = out_weight.shape[2] // parts
    merge = piece % 16 == 0

    def shifted(block, shift):
        if shift == 0:
            return block
        return lax.ppermute(block, "tp", [(i, (i + shift) % parts) for i in range(parts)])

    def all_parts(block, *earlier):
        if parts != 4:
            return [shifted(block, shift) for shift in range(parts)]
        one, three = shifted(block, 1), shifted(block, 3)
        from_left, from_right = one, three
        if earlier:
            from_left, from_right = lax.optimization_barrier((one, three) + earlier)[:2]
        rightwards = lax.ppermute(from_left, "tp", [(1, 2), (2, 3)])
        leftwards = lax.ppermute(from_right, "tp", [(1, 0), (2, 1)])
        return [block, one, jnp.where(me >= 2, rightwards, leftwards), three]

    def outgoing(layer, shift):
        target = lax.rem(me + shift, parts)
        return lax.dynamic_slice(
            qkv_weight, (layer, 0, target * block_width), (1, piece, block_width)
        )[0]

    source = lax.rem(me - jnp.arange(parts, dtype=jnp.int32) + parts, parts)
    seat = lax.axis_index("rep")
    by_links = merge and replicas == 8 and parts == 4 and layers == 2

    def after(array, *earlier):
        return lax.optimization_barrier((array,) + earlier)[0]

    def swapped(block, mask):
        return lax.ppermute(block, "rep", [(i, i ^ mask) for i in range(replicas)])

    def spread_first(block, *earlier):
        block = after(block, *earlier) if earlier else block
        return [(0, 0, block), (2, 0, swapped(block, 2)), (4, 0, swapped(block, 4))]

    def spread_second(spread):
        by_x, by_y = spread[1][2], spread[2][2]
        half = by_x.shape[0] // 2
        return spread + [(6, 0, swapped(by_x[:half], 4)), (6, half, swapped(by_y[half:], 2))]

    def listed(spreads, shifts):
        arrays, pieces, rows = [], [], []
        for spread, its_shifts in zip(spreads, shifts):
            for mask, first, array in spread:
                at = 0
                while at < array.shape[0]:
                    place, offset = divmod(first + at, piece)
                    count = min(piece - offset, array.shape[0] - at)
                    pieces.append((len(arrays), at, count, its_shifts[place]))
                    rows.append(((seat ^ mask) // 2) * piece + offset)
                    at += count
                arrays.append(array)
        return arrays, pieces, jnp.stack(rows).astype(jnp.int32)

    positions = lengths[None, :] + jnp.arange(step_count, dtype=jnp.int32)[:, None]
    half = head_dim // 2
    frequency = rope_base ** (-jnp.arange(half, dtype=jnp.float32) / half)
    angles = positions.astype(jnp.float32)[..., None] * frequency
    cosine, sine = jnp.cos(angles), jnp.sin(angles)
    cosine = jnp.concatenate([cosine, cosine], axis=-1)
    sine = jnp.concatenate([-sine, sine], axis=-1)

    gains = jnp.take(norm_gain.reshape(layers, replicas, parts, piece), source, axis=2)
    gains = jnp.moveaxis(gains, 2, 1).reshape(layers, parts, 1, slice_width)

    flat = inputs.reshape(flat_rows, model_width)
    blocks = split_parts(flat, source, parts, replicas, piece)
    hidden = [blocks[shift] for shift in range(parts)]

    def from_calls(layer):
        arrays = [
            lax.all_gather(shifted(outgoing(layer, shift), shift), "rep", axis=0, tiled=True)
            for shift in range(parts)
        ]
        pieces = [(shift, 0, slice_width, shift) for shift in range(parts)]
        return arrays, pieces, jnp.zeros((parts,), jnp.int32)

    def from_call(came):
        array = lax.all_gather(came, "rep", axis=0, tiled=True)
        pieces = [
            (0, (r * parts + shift) * piece, piece, shift)
            for r in range(replicas)
            for shift in range(parts)
        ]
        rows = jnp.array([r * piece for r in range(replicas) for _ in range(parts)], jnp.int32)
        return [array], pieces, rows

    stages = [[0, 1, 3], [2]]

    def row_scale(squares):
        return lax.rsqrt(squares / model_width + epsilon)

    if by_links:
        core = lax.rem(seat, 2)
        mine, theirs, squares = share_features(
            flat, jnp.full((1,), core, jnp.int32), replicas // 2
        )
        both = jnp.concatenate([mine, swapped(theirs, 1)], axis=0)
        both = split_parts(both, source, parts, replicas // 2, piece)
        both = [both[shift] for shift in range(parts)]
        other = swapped(squares.reshape(-1, 128), 1).reshape(flat_rows, 1)
        scale = row_scale(jnp.concatenate([squares, other], axis=0))
        core_gains = lax.dynamic_index_in_dim(
            gains[0].reshape(parts, replicas // 2, 2, piece), core, 2, keepdims=False
        ).reshape(parts, 1, slice_width // 2)
        one, three = shifted(outgoing(0, 1), 1), shifted(outgoing(0, 3), 3)
        two = shifted(after(outgoing(0, 2), one, three), 2)
        head = spread_first(outgoing(0, 0))
        body = spread_first(
            jnp.concatenate([one, three], axis=0), head[1][2], head[2][2]
        )
        head = spread_second(head)
        turned = [array for _, _, array in head[3:5]]
        tail = spread_first(two, body[1][2], body[2][2], *turned)
        ahead = [array for _, _, array in body[1:3]]
        across = [array for _, _, array in tail[1:3]]
        body = spread_second(body)
        turned += [array for _, _, array in body[3:5]]
        tail = spread_second(tail)
        gathers = [[listed([head, body], [[0], [1, 2]]), listed([tail], [[0]])]]
        later_two = shifted(after(outgoing(1, 2), two), 2)
        later_one = shifted(after(outgoing(1, 1), *across), 1)
        later_three = shifted(after(outgoing(1, 3), later_one), 3)
        came = (outgoing(1, 0), later_one, later_two, later_three)
        ready = (scale, core_gains, gathers[0][0][2], gathers[0][1][2], *both)
        sent = [after(out_weight[0], *across, *turned, later_two, *ready), out_weight[1]]
    else:
        gathers = [from_calls(layer) for layer in range(layers)]
        sent = [out_weight[layer] for layer in range(layers)]
    outs = [lax.all_gather(one, "rep", axis=0, tiled=True) for one in sent]

    columns = source * head_width
    for layer in range(layers):
        if by_links and layer == 0:
            mixed = None
            for stage, (arrays, pieces, rows) in zip(stages, gathers[0]):
                if mixed is not None:
                    mixed = lax.optimization_barrier(
                        (*mixed, later_one, later_two)
                    )[:2]
                mixed = project_qkv(
                    both, stage, core_gains, scale, arrays, pieces, rows, mixed, outputs=2
                )
            mixed = [mixed[0], swapped(mixed[1], 1)]
        else:
            mixed = project_qkv(
                hidden, list(range(parts)), gains[layer], None, *gathers[layer]
            )
        attended = attend(
            [one.reshape(step_count, row_count, block_width) for one in mixed],
            cosine,
            sine,
            query_gain[layer][None],
            key_gain[layer][None],
            stored_rotated_keys,
            stored_cache_values,
            lengths,
            layer,
        ).reshape(flat_rows, head_width)
        if by_links and layer == 0:
            came = lax.optimization_barrier((*came, attended))[:parts]
            gathers.append(from_call(jnp.concatenate(came, axis=0)))
            attended = all_parts(attended, outs[layer])
            own = project_out(attended, stages[0], outs[layer], columns)
            own = project_out(attended, stages[1], outs[layer], columns, own, hidden[0])
        else:
            own = project_out_whole(all_parts(attended), outs[layer], columns, hidden[0])
        hidden = all_parts(own)
    joined = join_parts(hidden, source, replicas, piece)
    return joined.reshape(step_count, row_count, model_width)


def solution(mesh):
    return jax.shard_map(
        on_device,
        mesh=mesh,
        in_specs=(
            P(None, "rep", None),
            P(None, ("rep", "tp"), None),
            P(None, ("rep", "tp"), None),
            P(),
            P(),
            P(),
            P(None, "rep", "tp", None, None),
            P(None, "rep", "tp", None, None),
            P("rep"),
        ),
        out_specs=P(None, "rep", None),
        check_vma=False,
    )
```

```python
import functools

import jax
import jax.numpy as jnp
from jax import lax
from jax.experimental import pallas as pl
from jax.experimental.pallas import tpu as pltpu
from jax.sharding import PartitionSpec as P

epsilon = 1e-06
rope_base = 1000000.0
MIB = 1024 * 1024
VMEM = pltpu.VMEM
SMEM = pltpu.SMEM


def vmem_spec():
    return pl.BlockSpec(memory_space=VMEM)


def smem_spec():
    return pl.BlockSpec(memory_space=SMEM)


def any_spec():
    return pl.BlockSpec(memory_space=pl.ANY)


def tiles(width, size=256):
    return [(start, min(size, width - start)) for start in range(0, width, size)]


def split_kernel(parts, replicas, piece, place_ref, whole_ref, blocks_ref):
    for part in range(parts):
        columns = [
            whole_ref[:, (r * parts + part) * piece : (r * parts + part + 1) * piece]
            for r in range(replicas)
        ]
        blocks_ref[place_ref[part]] = jnp.concatenate(columns, axis=1)


def split_parts(whole, place, parts, replicas, piece):
    rows = whole.shape[0]
    return pl.pallas_call(
        functools.partial(split_kernel, parts, replicas, piece),
        out_shape=jax.ShapeDtypeStruct((parts, rows, replicas * piece), whole.dtype),
        in_specs=[smem_spec(), vmem_spec()],
        out_specs=vmem_spec(),
        compiler_params=pltpu.CompilerParams(vmem_limit_bytes=24 * MIB),
    )(place, whole)


def share_kernel(shares, core_ref, whole_ref, mine_ref, theirs_ref, squares_ref):
    width = mine_ref.shape[1] // shares
    core = core_ref[0]
    squares = None
    for share in range(shares):
        columns = slice(share * width, (share + 1) * width)
        for whose, to_ref in ((core, mine_ref), (1 - core, theirs_ref)):
            start = pl.multiple_of((2 * share + whose) * width, 128)
            some = whole_ref[:, pl.ds(start, width)]
            to_ref[:, columns] = some
            wide = some.astype(jnp.float32)
            term = jnp.sum(wide * wide, axis=1, keepdims=True)
            squares = term if squares is None else squares + term
    squares_ref[...] = squares


def share_features(whole, core, shares):
    rows, width = whole.shape
    part = jax.ShapeDtypeStruct((rows, width // 2), whole.dtype)
    return pl.pallas_call(
        functools.partial(share_kernel, shares),
        out_shape=(part, part, jax.ShapeDtypeStruct((rows, 1), jnp.float32)),
        in_specs=[smem_spec(), vmem_spec()],
        out_specs=(vmem_spec(), vmem_spec(), vmem_spec()),
        compiler_params=pltpu.CompilerParams(vmem_limit_bytes=24 * MIB),
    )(core, whole)


def join_kernel(parts, replicas, piece, place_ref, *refs):
    block_refs, whole_ref, held, sems = refs[:parts], refs[parts], refs[parts + 1], refs[parts + 2]
    copies = [
        pltpu.make_async_copy(block_refs[shift], held.at[place_ref[shift]], sems.at[shift])
        for shift in range(parts)
    ]
    for copy in copies:
        copy.start()
    for copy in copies:
        copy.wait()
    for r in range(replicas):
        columns = [held[part, :, r * piece : (r + 1) * piece] for part in range(parts)]
        whole_ref[:, r * parts * piece : (r + 1) * parts * piece] = jnp.concatenate(columns, axis=1)


def join_parts(blocks, place, replicas, piece):
    parts = len(blocks)
    rows = blocks[0].shape[0]
    return pl.pallas_call(
        functools.partial(join_kernel, parts, replicas, piece),
        out_shape=jax.ShapeDtypeStruct((rows, parts * replicas * piece), blocks[0].dtype),
        in_specs=[smem_spec()] + [any_spec()] * parts,
        out_specs=vmem_spec(),
        scratch_shapes=[
            VMEM((parts, rows, replicas * piece), blocks[0].dtype),
            pltpu.SemaphoreType.DMA((parts,)),
        ],
        compiler_params=pltpu.CompilerParams(vmem_limit_bytes=24 * MIB),
    )(place, *blocks)


def qkv_kernel(count, shifts, pieces, arrays, scaled, continued, rows_ref, *refs):
    block_refs, refs = refs[:count], refs[count:]
    gain_ref, refs = refs[0], refs[1:]
    if scaled:
        scale_ref, refs = refs[0], refs[1:]
    weight_refs, refs = refs[:arrays], refs[arrays:]
    outputs = (len(refs) - 3) // (2 if continued else 1)
    if continued:
        before_refs, refs = refs[:outputs], refs[outputs:]
    mixed_refs, refs = refs[:outputs], refs[outputs:]
    held, normed, sems = refs
    each = mixed_refs[0].shape[0]
    copies = []
    for index, (array, first, size, place) in enumerate(pieces):
        to = pl.multiple_of(rows_ref[index], 16)
        copies.append(
            pltpu.make_async_copy(
                weight_refs[array].at[pl.ds(first, size)],
                held.at[place, pl.ds(to, size)],
                sems.at[index],
            )
        )
        copies[-1].start()
    step = 32

    @pl.loop(0, normed.shape[1] // step)
    def _(tile):
        rows = pl.ds(pl.multiple_of(tile * step, step), step)
        if scaled:
            scale = scale_ref[rows, :]
        else:
            squares = None
            for ref in block_refs:
                wide = ref[rows, :].astype(jnp.float32)
                term = jnp.sum(wide * wide, axis=-1, keepdims=True)
                squares = term if squares is None else squares + term
            scale = lax.rsqrt(squares / (count * normed.shape[2]) + epsilon)
        for place, shift in enumerate(shifts):
            wide = block_refs[place][rows, :].astype(jnp.float32)
            normed[place, rows, :] = (wide * scale * gain_ref[shift]).astype(jnp.bfloat16)

    for place in range(count):
        for index in range(len(pieces)):
            if pieces[index][3] == place:
                copies[index].wait()
        for start, size in tiles(mixed_refs[0].shape[1]):
            columns = slice(start, start + size)
            terms = jnp.dot(
                normed[place], held[place, :, columns], preferred_element_type=jnp.float32
            )
            for index in range(outputs):
                term = terms[index * each : (index + 1) * each]
                if place > 0:
                    mixed_refs[index][:, columns] += term
                elif continued:
                    mixed_refs[index][:, columns] = before_refs[index][:, columns] + term
                else:
                    mixed_refs[index][:, columns] = term


def project_qkv(
    blocks, shifts, gains, scale, weights, pieces, rows, before=None, outputs=1
):
    count = len(shifts)
    row_total, width = blocks[0].shape
    columns = weights[0].shape[1]
    continued = before is not None
    scaled = scale is not None
    operands = [rows] + [blocks[shift] for shift in shifts] + [gains] + [scale] * scaled
    in_specs = [smem_spec()] + [vmem_spec()] * (len(operands) - 1) + [any_spec()] * len(weights)
    operands += list(weights)
    if continued:
        operands += list(before)
        in_specs += [vmem_spec()] * outputs
    mixed = jax.ShapeDtypeStruct((row_total // outputs, columns), jnp.float32)
    return pl.pallas_call(
        functools.partial(
            qkv_kernel, count, shifts, pieces, len(weights), scaled, continued
        ),
        out_shape=[mixed] * outputs,
        in_specs=in_specs,
        out_specs=[vmem_spec()] * outputs,
        scratch_shapes=[
            VMEM((count, width, columns), jnp.bfloat16),
            VMEM((count, row_total, width), jnp.bfloat16),
            pltpu.SemaphoreType.DMA((len(pieces),)),
        ],
        compiler_params=pltpu.CompilerParams(vmem_limit_bytes=(52 if scaled else 40) * MIB),
        cost_estimate=pl.CostEstimate(
            flops=2 * row_total * count * width * columns,
            bytes_accessed=2 * count * width * columns,
            transcendentals=0,
        ),
    )(*operands)


def whole_out_kernel(count, column_ref, *refs):
    attended_refs, refs = refs[:count], refs[count:]
    weight_ref, residual_ref, hidden_ref, held, total, sems = refs
    width = attended_refs[0].shape[1]
    copies = []
    for shift in range(count):
        start = pl.multiple_of(column_ref[shift], 128)
        copies.append(
            pltpu.make_async_copy(
                weight_ref.at[:, pl.ds(start, width)], held.at[shift], sems.at[shift]
            )
        )
        copies[-1].start()
    for shift in range(count):
        copies[shift].wait()
        for start, size in tiles(hidden_ref.shape[1]):
            features = slice(start, start + size)
            term = lax.dot_general(
                attended_refs[shift][...],
                held[shift, features, :],
                (((1,), (1,)), ((), ())),
                preferred_element_type=jnp.float32,
            )
            if shift > 0:
                term = total[:, features] + term
            if shift < count - 1:
                total[:, features] = term
            else:
                hidden_ref[:, features] = (
                    residual_ref[:, features].astype(jnp.float32) + term
                ).astype(hidden_ref.dtype)


def project_out_whole(attended, weight, columns, residual):
    count = len(attended)
    row_total, width = attended[0].shape
    features = weight.shape[0]
    return pl.pallas_call(
        functools.partial(whole_out_kernel, count),
        out_shape=jax.ShapeDtypeStruct((row_total, features), residual.dtype),
        in_specs=[smem_spec()] + [vmem_spec()] * count + [any_spec(), vmem_spec()],
        out_specs=vmem_spec(),
        scratch_shapes=[
            VMEM((count, features, width), jnp.bfloat16),
            VMEM((row_total, features), jnp.float32),
            pltpu.SemaphoreType.DMA((count,)),
        ],
        compiler_params=pltpu.CompilerParams(vmem_limit_bytes=50 * MIB),
        cost_estimate=pl.CostEstimate(
            flops=2 * row_total * count * width * features,
            bytes_accessed=2 * count * width * features,
            transcendentals=0,
        ),
    )(columns, *attended, weight, residual)


def out_kernel(count, shifts, column_ref, *refs):
    attended_refs, refs = refs[:count], refs[count:]
    weight_ref, refs = refs[0], refs[1:]
    last = len(refs) > 3
    if last:
        before_ref, residual_ref, refs = refs[0], refs[1], refs[2:]
    sum_ref, held, sems = refs[0], refs[-2], refs[-1]
    width = attended_refs[0].shape[1]
    copies = []
    for place, shift in enumerate(shifts):
        start = pl.multiple_of(column_ref[shift], 128)
        copies.append(
            pltpu.make_async_copy(
                weight_ref.at[:, pl.ds(start, width)], held.at[place], sems.at[place]
            )
        )
        copies[-1].start()
    for place in range(count):
        copies[place].wait()
        for start, size in tiles(sum_ref.shape[1]):
            features = slice(start, start + size)
            term = lax.dot_general(
                attended_refs[place][...],
                held[place, features, :],
                (((1,), (1,)), ((), ())),
                preferred_element_type=jnp.float32,
            )
            if last:
                total = before_ref[:, features] + term
                total = residual_ref[:, features].astype(jnp.float32) + total
                sum_ref[:, features] = total.astype(sum_ref.dtype)
            elif place > 0:
                sum_ref[:, features] += term
            else:
                sum_ref[:, features] = term


def project_out(attended, shifts, weight, columns, before=None, residual=None):
    count = len(shifts)
    row_total, width = attended[0].shape
    features = weight.shape[0]
    last = residual is not None
    operands = [columns] + [attended[shift] for shift in shifts] + [weight]
    in_specs = [smem_spec()] + [vmem_spec()] * count + [any_spec()]
    if last:
        operands += [before, residual]
        in_specs += [vmem_spec()] * 2
    return pl.pallas_call(
        functools.partial(out_kernel, count, shifts),
        out_shape=jax.ShapeDtypeStruct(
            (row_total, features), residual.dtype if last else jnp.float32
        ),
        in_specs=in_specs,
        out_specs=vmem_spec(),
        scratch_shapes=[
            VMEM((count, features, width), jnp.bfloat16),
            pltpu.SemaphoreType.DMA((count,)),
        ],
        compiler_params=pltpu.CompilerParams(vmem_limit_bytes=50 * MIB),
        cost_estimate=pl.CostEstimate(
            flops=2 * row_total * count * width * features,
            bytes_accessed=2 * count * width * features,
            transcendentals=0,
        ),
    )(*operands)


def attention_kernel(heads, lengths_ref, *refs):
    mixed_refs, refs = refs[:-9], refs[-9:]
    cosine_ref, sine_ref, query_gain_ref, key_gain_ref, keys_ref, values_ref = refs[:6]
    attended_ref, query_rows, result_rows = refs[6:]
    steps, rows, _ = mixed_refs[0].shape
    slots, size = keys_ref.shape[-2:]
    step_rows = steps * rows
    per_row = heads * steps
    first_row = pl.program_id(0) * rows
    scale = size ** (-0.5)
    cosine = cosine_ref[...]
    sine = sine_ref[...]

    def projected(vector):
        columns = slice(vector * size, (vector + 1) * size)
        return sum(ref[:, :, columns] for ref in mixed_refs)

    def turned(vectors, gain):
        mean = jnp.mean(vectors * vectors, axis=-1, keepdims=True)
        normal = vectors * lax.rsqrt(mean + epsilon) * gain
        swapped = jnp.concatenate([normal[..., size // 2 :], normal[..., : size // 2]], axis=-1)
        return normal * cosine + swapped * sine

    for head in range(heads):
        vectors = projected(head)
        query = turned(vectors, query_gain_ref[...])
        query_rows[head * step_rows : (head + 1) * step_rows, :] = query.reshape(step_rows, size)
    new_key = turned(projected(heads), key_gain_ref[...])
    new_key = new_key.reshape(step_rows, size).astype(jnp.bfloat16)
    new_value = projected(heads + 1)
    new_value = new_value.reshape(step_rows, size).astype(jnp.bfloat16)

    queries = [
        query_rows[pl.ds(r, per_row, stride=rows), :].astype(jnp.bfloat16) for r in range(rows)
    ]
    nt = (((1,), (1,)), ((), ()))
    column = lax.broadcasted_iota(jnp.int32, (per_row, slots), 1)
    old = []
    for r in range(rows):
        score = lax.dot_general(
            queries[r], keys_ref[r], nt, preferred_element_type=jnp.float32
        )
        old.append(jnp.where(column < lengths_ref[first_row + r], score * scale, -jnp.inf))
    old = jnp.concatenate(old, axis=0)
    new = lax.dot_general(
        jnp.concatenate(queries, axis=0), new_key, nt, preferred_element_type=jnp.float32
    )
    at = lax.broadcasted_iota(jnp.int32, (rows * per_row, step_rows), 0)
    to = lax.broadcasted_iota(jnp.int32, (rows * per_row, step_rows), 1)
    seen = (at // per_row == to % rows) & (to // rows <= at % steps)
    new = jnp.where(seen, new * scale, -jnp.inf)
    highest = jnp.maximum(
        jnp.max(old, axis=-1, keepdims=True), jnp.max(new, axis=-1, keepdims=True)
    )
    old = jnp.exp(old - highest)
    new = jnp.exp(new - highest)
    total = jnp.sum(old, axis=-1, keepdims=True) + jnp.sum(new, axis=-1, keepdims=True)
    old = (old / total).astype(jnp.bfloat16)
    new = (new / total).astype(jnp.bfloat16)
    from_new = jnp.dot(new, new_value, preferred_element_type=jnp.float32)
    for r in range(rows):
        part = slice(r * per_row, (r + 1) * per_row)
        result = jnp.dot(old[part], values_ref[r], preferred_element_type=jnp.float32)
        result_rows[pl.ds(r, per_row, stride=rows), :] = result + from_new[part]
    for head in range(heads):
        result = result_rows[head * step_rows : (head + 1) * step_rows, :]
        attended_ref[:, :, head * size : (head + 1) * size] = result.reshape(
            steps, rows, size
        ).astype(jnp.bfloat16)


def attend(mixed, cosine, sine, query_gain, key_gain, keys, values, lengths, layer):
    steps, row_total, columns = mixed[0].shape
    groups, slots, size = keys.shape[2:]
    per_group = columns // (groups * size)
    heads = per_group - 2
    rows = 16
    cache_spec = pl.BlockSpec(
        (None, rows, None, slots, size), lambda i, g, _: (layer, i, g, 0, 0)
    )
    turn_spec = pl.BlockSpec((steps, rows, size), lambda i, g, _: (0, i, 0))
    gain_spec = pl.BlockSpec((1, size), lambda i, g, _: (0, 0))
    return pl.pallas_call(
        functools.partial(attention_kernel, heads),
        out_shape=jax.ShapeDtypeStruct((steps, row_total, groups * heads * size), jnp.bfloat16),
        grid_spec=pltpu.PrefetchScalarGridSpec(
            num_scalar_prefetch=1,
            grid=(row_total // rows, groups),
            in_specs=[pl.BlockSpec((steps, rows, per_group * size), lambda i, g, _: (0, i, g))]
            * len(mixed)
            + [
                turn_spec,
                turn_spec,
                gain_spec,
                gain_spec,
                cache_spec,
                cache_spec,
            ],
            out_specs=pl.BlockSpec((steps, rows, heads * size), lambda i, g, _: (0, i, g)),
            scratch_shapes=[
                VMEM((heads * steps * rows, size), jnp.float32),
                VMEM((heads * steps * rows, size), jnp.float32),
            ],
        ),
        compiler_params=pltpu.CompilerParams(vmem_limit_bytes=49 * MIB),
        cost_estimate=pl.CostEstimate(
            flops=4 * row_total * groups * heads * steps * slots * size,
            bytes_accessed=4 * row_total * groups * slots * size,
            transcendentals=row_total * groups * heads * steps * slots,
        ),
    )(lengths, *mixed, cosine, sine, query_gain, key_gain, keys, values)


def on_device(
    inputs,
    qkv_weight,
    out_weight,
    norm_gain,
    query_gain,
    key_gain,
    stored_rotated_keys,
    stored_cache_values,
    lengths,
):
    step_count, row_count, model_width = inputs.shape
    flat_rows = step_count * row_count
    layers = qkv_weight.shape[0]
    head_dim = stored_rotated_keys.shape[4]
    parts = lax.axis_size("tp")
    replicas = lax.axis_size("rep")
    me = lax.axis_index("tp")
    piece = qkv_weight.shape[1]
    slice_width = replicas * piece
    block_width = qkv_weight.shape[2] // parts
    head_width = out_weight.shape[2] // parts
    merge = piece % 16 == 0

    def shifted(block, shift):
        if shift == 0:
            return block
        return lax.ppermute(block, "tp", [(i, (i + shift) % parts) for i in range(parts)])

    def all_parts(block, *earlier):
        if parts != 4:
            return [shifted(block, shift) for shift in range(parts)]
        one, three = shifted(block, 1), shifted(block, 3)
        from_left, from_right = one, three
        if earlier:
            from_left, from_right = lax.optimization_barrier((one, three) + earlier)[:2]
        rightwards = lax.ppermute(from_left, "tp", [(1, 2), (2, 3)])
        leftwards = lax.ppermute(from_right, "tp", [(1, 0), (2, 1)])
        return [block, one, jnp.where(me >= 2, rightwards, leftwards), three]

    def outgoing(layer, shift):
        target = lax.rem(me + shift, parts)
        return lax.dynamic_slice(
            qkv_weight, (layer, 0, target * block_width), (1, piece, block_width)
        )[0]

    source = lax.rem(me - jnp.arange(parts, dtype=jnp.int32) + parts, parts)
    seat = lax.axis_index("rep")
    by_links = merge and replicas == 8 and parts == 4 and layers == 2

    def after(array, *earlier):
        return lax.optimization_barrier((array,) + earlier)[0]

    def swapped(block, mask):
        return lax.ppermute(block, "rep", [(i, i ^ mask) for i in range(replicas)])

    def spread_first(block, *earlier):
        block = after(block, *earlier) if earlier else block
        return [(0, 0, block), (2, 0, swapped(block, 2)), (4, 0, swapped(block, 4))]

    def spread_second(spread):
        by_x, by_y = spread[1][2], spread[2][2]
        half = by_x.shape[0] // 2
        return spread + [(6, 0, swapped(by_x[:half], 4)), (6, half, swapped(by_y[half:], 2))]

    def listed(spreads, shifts):
        arrays, pieces, rows = [], [], []
        for spread, its_shifts in zip(spreads, shifts):
            for mask, first, array in spread:
                at = 0
                while at < array.shape[0]:
                    place, offset = divmod(first + at, piece)
                    count = min(piece - offset, array.shape[0] - at)
                    pieces.append((len(arrays), at, count, its_shifts[place]))
                    rows.append(((seat ^ mask) // 2) * piece + offset)
                    at += count
                arrays.append(array)
        return arrays, pieces, jnp.stack(rows).astype(jnp.int32)

    positions = lengths[None, :] + jnp.arange(step_count, dtype=jnp.int32)[:, None]
    half = head_dim // 2
    frequency = rope_base ** (-jnp.arange(half, dtype=jnp.float32) / half)
    angles = positions.astype(jnp.float32)[..., None] * frequency
    cosine, sine = jnp.cos(angles), jnp.sin(angles)
    cosine = jnp.concatenate([cosine, cosine], axis=-1)
    sine = jnp.concatenate([-sine, sine], axis=-1)

    gains = jnp.take(norm_gain.reshape(layers, replicas, parts, piece), source, axis=2)
    gains = jnp.moveaxis(gains, 2, 1).reshape(layers, parts, 1, slice_width)

    flat = inputs.reshape(flat_rows, model_width)
    blocks = split_parts(flat, source, parts, replicas, piece)
    hidden = [blocks[shift] for shift in range(parts)]

    def from_calls(layer):
        arrays = [
            lax.all_gather(shifted(outgoing(layer, shift), shift), "rep", axis=0, tiled=True)
            for shift in range(parts)
        ]
        pieces = [(shift, 0, slice_width, shift) for shift in range(parts)]
        return arrays, pieces, jnp.zeros((parts,), jnp.int32)

    def from_call(came):
        array = lax.all_gather(came, "rep", axis=0, tiled=True)
        pieces = [
            (0, (r * parts + shift) * piece, piece, shift)
            for r in range(replicas)
            for shift in range(parts)
        ]
        rows = jnp.array([r * piece for r in range(replicas) for _ in range(parts)], jnp.int32)
        return [array], pieces, rows

    stages = [[0, 1, 3], [2]]

    def row_scale(squares):
        return lax.rsqrt(squares / model_width + epsilon)

    if by_links:
        core = lax.rem(seat, 2)
        mine, theirs, squares = share_features(
            flat, jnp.full((1,), core, jnp.int32), replicas // 2
        )
        swapped_share = swapped(theirs, 1)
        both = jnp.concatenate([mine, swapped_share], axis=0)
        both = split_parts(both, source, parts, replicas // 2, piece)
        both = [both[shift] for shift in range(parts)]
        other = swapped(squares.reshape(-1, 128), 1).reshape(flat_rows, 1)
        scale = row_scale(jnp.concatenate([squares, other], axis=0))
        core_gains = lax.dynamic_index_in_dim(
            gains[0].reshape(parts, replicas // 2, 2, piece), core, 2, keepdims=False
        ).reshape(parts, 1, slice_width // 2)
        one, three = shifted(outgoing(0, 1), 1), shifted(outgoing(0, 3), 3)
        two = shifted(after(outgoing(0, 2), one, three, swapped_share), 2)
        head = spread_first(outgoing(0, 0))
        body = spread_first(
            jnp.concatenate([one, three], axis=0), head[1][2], head[2][2]
        )
        head = spread_second(head)
        turned = [array for _, _, array in head[3:5]]
        tail = spread_first(two, body[1][2], body[2][2], *turned)
        ahead = [array for _, _, array in body[1:3]]
        across = [array for _, _, array in tail[1:3]]
        body = spread_second(body)
        tail = spread_second(tail)
        gathers = [[listed([head, body], [[0], [1, 2]]), listed([tail], [[0]])]]
        later_one = shifted(after(outgoing(1, 1), two), 1)
        later_two = shifted(after(outgoing(1, 2), *across), 2)
        later_three = shifted(after(outgoing(1, 3), later_two), 3)
        came = (outgoing(1, 0), later_one, later_two, later_three)
        ready = (scale, core_gains, gathers[0][0][2], gathers[0][1][2], *both)
        sent = [after(out_weight[0], *across, *turned, later_one, *ready), out_weight[1]]
    else:
        gathers = [from_calls(layer) for layer in range(layers)]
        sent = [out_weight[layer] for layer in range(layers)]
    outs = [lax.all_gather(one, "rep", axis=0, tiled=True) for one in sent]

    columns = source * head_width
    for layer in range(layers):
        if by_links and layer == 0:
            mixed = None
            for stage, (arrays, pieces, rows) in zip(stages, gathers[0]):
                if mixed is not None:
                    mixed = lax.optimization_barrier(
                        (*mixed, later_one, later_two)
                    )[:2]
                mixed = project_qkv(
                    both, stage, core_gains, scale, arrays, pieces, rows, mixed, outputs=2
                )
            mixed = [mixed[0], swapped(mixed[1], 1)]
        else:
            mixed = project_qkv(
                hidden, list(range(parts)), gains[layer], None, *gathers[layer]
            )
        attended = attend(
            [one.reshape(step_count, row_count, block_width) for one in mixed],
            cosine,
            sine,
            query_gain[layer][None],
            key_gain[layer][None],
            stored_rotated_keys,
            stored_cache_values,
            lengths,
            layer,
        ).reshape(flat_rows, head_width)
        if by_links and layer == 0:
            came = lax.optimization_barrier((*came, attended))[:parts]
            gathers.append(from_call(jnp.concatenate(came, axis=0)))
            attended = all_parts(attended, outs[layer])
            own = project_out(attended, stages[0], outs[layer], columns)
            own = project_out(attended, stages[1], outs[layer], columns, own, hidden[0])
        else:
            own = project_out_whole(all_parts(attended), outs[layer], columns, hidden[0])
        hidden = all_parts(own)
    joined = join_parts(hidden, source, replicas, piece)
    return joined.reshape(step_count, row_count, model_width)


def solution(mesh):
    return jax.shard_map(
        on_device,
        mesh=mesh,
        in_specs=(
            P(None, "rep", None),
            P(None, ("rep", "tp"), None),
            P(None, ("rep", "tp"), None),
            P(),
            P(),
            P(),
            P(None, "rep", "tp", None, None),
            P(None, "rep", "tp", None, None),
            P("rep"),
        ),
        out_specs=P(None, "rep", None),
        check_vma=False,
    )
```

```python
import functools

import jax
import jax.numpy as jnp
from jax import lax
from jax.experimental import pallas as pl
from jax.experimental.pallas import tpu as pltpu
from jax.sharding import PartitionSpec as P

epsilon = 1e-06
rope_base = 1000000.0
MIB = 1024 * 1024
VMEM = pltpu.VMEM
SMEM = pltpu.SMEM


def vmem_spec():
    return pl.BlockSpec(memory_space=VMEM)


def smem_spec():
    return pl.BlockSpec(memory_space=SMEM)


def any_spec():
    return pl.BlockSpec(memory_space=pl.ANY)


def tiles(width, size=256):
    return [(start, min(size, width - start)) for start in range(0, width, size)]


def split_kernel(parts, replicas, piece, place_ref, whole_ref, blocks_ref):
    for part in range(parts):
        columns = [
            whole_ref[:, (r * parts + part) * piece : (r * parts + part + 1) * piece]
            for r in range(replicas)
        ]
        blocks_ref[place_ref[part]] = jnp.concatenate(columns, axis=1)


def split_parts(whole, place, parts, replicas, piece):
    rows = whole.shape[0]
    return pl.pallas_call(
        functools.partial(split_kernel, parts, replicas, piece),
        out_shape=jax.ShapeDtypeStruct((parts, rows, replicas * piece), whole.dtype),
        in_specs=[smem_spec(), vmem_spec()],
        out_specs=vmem_spec(),
        compiler_params=pltpu.CompilerParams(vmem_limit_bytes=24 * MIB),
    )(place, whole)


def share_kernel(shares, core_ref, whole_ref, mine_ref, theirs_ref, squares_ref):
    width = mine_ref.shape[1] // shares
    core = core_ref[0]
    squares = None
    for share in range(shares):
        columns = slice(share * width, (share + 1) * width)
        for whose, to_ref in ((core, mine_ref), (1 - core, theirs_ref)):
            start = pl.multiple_of((2 * share + whose) * width, 128)
            some = whole_ref[:, pl.ds(start, width)]
            to_ref[:, columns] = some
            wide = some.astype(jnp.float32)
            term = jnp.sum(wide * wide, axis=1, keepdims=True)
            squares = term if squares is None else squares + term
    squares_ref[...] = squares


def share_features(whole, core, shares):
    rows, width = whole.shape
    part = jax.ShapeDtypeStruct((rows, width // 2), whole.dtype)
    return pl.pallas_call(
        functools.partial(share_kernel, shares),
        out_shape=(part, part, jax.ShapeDtypeStruct((rows, 1), jnp.float32)),
        in_specs=[smem_spec(), vmem_spec()],
        out_specs=(vmem_spec(), vmem_spec(), vmem_spec()),
        compiler_params=pltpu.CompilerParams(vmem_limit_bytes=24 * MIB),
    )(core, whole)


def join_kernel(parts, replicas, piece, place_ref, *refs):
    block_refs, whole_ref, held, sems = refs[:parts], refs[parts], refs[parts + 1], refs[parts + 2]
    copies = [
        pltpu.make_async_copy(block_refs[shift], held.at[place_ref[shift]], sems.at[shift])
        for shift in range(parts)
    ]
    for copy in copies:
        copy.start()
    for copy in copies:
        copy.wait()
    for r in range(replicas):
        columns = [held[part, :, r * piece : (r + 1) * piece] for part in range(parts)]
        whole_ref[:, r * parts * piece : (r + 1) * parts * piece] = jnp.concatenate(columns, axis=1)


def join_parts(blocks, place, replicas, piece):
    parts = len(blocks)
    rows = blocks[0].shape[0]
    return pl.pallas_call(
        functools.partial(join_kernel, parts, replicas, piece),
        out_shape=jax.ShapeDtypeStruct((rows, parts * replicas * piece), blocks[0].dtype),
        in_specs=[smem_spec()] + [any_spec()] * parts,
        out_specs=vmem_spec(),
        scratch_shapes=[
            VMEM((parts, rows, replicas * piece), blocks[0].dtype),
            pltpu.SemaphoreType.DMA((parts,)),
        ],
        compiler_params=pltpu.CompilerParams(vmem_limit_bytes=24 * MIB),
    )(place, *blocks)


def qkv_kernel(count, shifts, pieces, arrays, scaled, continued, rows_ref, *refs):
    block_refs, refs = refs[:count], refs[count:]
    gain_ref, refs = refs[0], refs[1:]
    if scaled:
        scale_ref, refs = refs[0], refs[1:]
    weight_refs, refs = refs[:arrays], refs[arrays:]
    outputs = (len(refs) - 3) // (2 if continued else 1)
    if continued:
        before_refs, refs = refs[:outputs], refs[outputs:]
    mixed_refs, refs = refs[:outputs], refs[outputs:]
    held, normed, sems = refs
    each = mixed_refs[0].shape[0]
    copies = []
    for index, (array, first, size, place) in enumerate(pieces):
        to = pl.multiple_of(rows_ref[index], 16)
        copies.append(
            pltpu.make_async_copy(
                weight_refs[array].at[pl.ds(first, size)],
                held.at[place, pl.ds(to, size)],
                sems.at[index],
            )
        )
        copies[-1].start()
    step = 32

    @pl.loop(0, normed.shape[1] // step)
    def _(tile):
        rows = pl.ds(pl.multiple_of(tile * step, step), step)
        if scaled:
            scale = scale_ref[rows, :]
        else:
            squares = None
            for ref in block_refs:
                wide = ref[rows, :].astype(jnp.float32)
                term = jnp.sum(wide * wide, axis=-1, keepdims=True)
                squares = term if squares is None else squares + term
            scale = lax.rsqrt(squares / (count * normed.shape[2]) + epsilon)
        for place, shift in enumerate(shifts):
            wide = block_refs[place][rows, :].astype(jnp.float32)
            normed[place, rows, :] = (wide * scale * gain_ref[shift]).astype(jnp.bfloat16)

    for place in range(count):
        for index in range(len(pieces)):
            if pieces[index][3] == place:
                copies[index].wait()
        for start, size in tiles(mixed_refs[0].shape[1]):
            columns = slice(start, start + size)
            terms = jnp.dot(
                normed[place], held[place, :, columns], preferred_element_type=jnp.float32
            )
            for index in range(outputs):
                term = terms[index * each : (index + 1) * each]
                if place > 0:
                    mixed_refs[index][:, columns] += term
                elif continued:
                    mixed_refs[index][:, columns] = before_refs[index][:, columns] + term
                else:
                    mixed_refs[index][:, columns] = term


def project_qkv(
    blocks, shifts, gains, scale, weights, pieces, rows, before=None, outputs=1
):
    count = len(shifts)
    row_total, width = blocks[0].shape
    columns = weights[0].shape[1]
    continued = before is not None
    scaled = scale is not None
    operands = [rows] + [blocks[shift] for shift in shifts] + [gains] + [scale] * scaled
    in_specs = [smem_spec()] + [vmem_spec()] * (len(operands) - 1) + [any_spec()] * len(weights)
    operands += list(weights)
    if continued:
        operands += list(before)
        in_specs += [vmem_spec()] * outputs
    mixed = jax.ShapeDtypeStruct((row_total // outputs, columns), jnp.float32)
    return pl.pallas_call(
        functools.partial(
            qkv_kernel, count, shifts, pieces, len(weights), scaled, continued
        ),
        out_shape=[mixed] * outputs,
        in_specs=in_specs,
        out_specs=[vmem_spec()] * outputs,
        scratch_shapes=[
            VMEM((count, width, columns), jnp.bfloat16),
            VMEM((count, row_total, width), jnp.bfloat16),
            pltpu.SemaphoreType.DMA((len(pieces),)),
        ],
        compiler_params=pltpu.CompilerParams(vmem_limit_bytes=(52 if scaled else 40) * MIB),
        cost_estimate=pl.CostEstimate(
            flops=2 * row_total * count * width * columns,
            bytes_accessed=2 * count * width * columns,
            transcendentals=0,
        ),
    )(*operands)


def whole_out_kernel(count, column_ref, *refs):
    attended_refs, refs = refs[:count], refs[count:]
    weight_ref, residual_ref, hidden_ref, held, total, sems = refs
    width = attended_refs[0].shape[1]
    copies = []
    for shift in range(count):
        start = pl.multiple_of(column_ref[shift], 128)
        copies.append(
            pltpu.make_async_copy(
                weight_ref.at[:, pl.ds(start, width)], held.at[shift], sems.at[shift]
            )
        )
        copies[-1].start()
    for shift in range(count):
        copies[shift].wait()
        for start, size in tiles(hidden_ref.shape[1]):
            features = slice(start, start + size)
            term = lax.dot_general(
                attended_refs[shift][...],
                held[shift, features, :],
                (((1,), (1,)), ((), ())),
                preferred_element_type=jnp.float32,
            )
            if shift > 0:
                term = total[:, features] + term
            if shift < count - 1:
                total[:, features] = term
            else:
                hidden_ref[:, features] = (
                    residual_ref[:, features].astype(jnp.float32) + term
                ).astype(hidden_ref.dtype)


def project_out_whole(attended, weight, columns, residual):
    count = len(attended)
    row_total, width = attended[0].shape
    features = weight.shape[0]
    return pl.pallas_call(
        functools.partial(whole_out_kernel, count),
        out_shape=jax.ShapeDtypeStruct((row_total, features), residual.dtype),
        in_specs=[smem_spec()] + [vmem_spec()] * count + [any_spec(), vmem_spec()],
        out_specs=vmem_spec(),
        scratch_shapes=[
            VMEM((count, features, width), jnp.bfloat16),
            VMEM((row_total, features), jnp.float32),
            pltpu.SemaphoreType.DMA((count,)),
        ],
        compiler_params=pltpu.CompilerParams(vmem_limit_bytes=50 * MIB),
        cost_estimate=pl.CostEstimate(
            flops=2 * row_total * count * width * features,
            bytes_accessed=2 * count * width * features,
            transcendentals=0,
        ),
    )(columns, *attended, weight, residual)


def out_kernel(count, shifts, column_ref, *refs):
    attended_refs, refs = refs[:count], refs[count:]
    weight_ref, refs = refs[0], refs[1:]
    last = len(refs) > 3
    if last:
        before_ref, residual_ref, refs = refs[0], refs[1], refs[2:]
    sum_ref, held, sems = refs[0], refs[-2], refs[-1]
    width = attended_refs[0].shape[1]
    copies = []
    for place, shift in enumerate(shifts):
        start = pl.multiple_of(column_ref[shift], 128)
        copies.append(
            pltpu.make_async_copy(
                weight_ref.at[:, pl.ds(start, width)], held.at[place], sems.at[place]
            )
        )
        copies[-1].start()
    for place in range(count):
        copies[place].wait()
        for start, size in tiles(sum_ref.shape[1]):
            features = slice(start, start + size)
            term = lax.dot_general(
                attended_refs[place][...],
                held[place, features, :],
                (((1,), (1,)), ((), ())),
                preferred_element_type=jnp.float32,
            )
            if last:
                total = before_ref[:, features] + term
                total = residual_ref[:, features].astype(jnp.float32) + total
                sum_ref[:, features] = total.astype(sum_ref.dtype)
            elif place > 0:
                sum_ref[:, features] += term
            else:
                sum_ref[:, features] = term


def project_out(attended, shifts, weight, columns, before=None, residual=None):
    count = len(shifts)
    row_total, width = attended[0].shape
    features = weight.shape[0]
    last = residual is not None
    operands = [columns] + [attended[shift] for shift in shifts] + [weight]
    in_specs = [smem_spec()] + [vmem_spec()] * count + [any_spec()]
    if last:
        operands += [before, residual]
        in_specs += [vmem_spec()] * 2
    return pl.pallas_call(
        functools.partial(out_kernel, count, shifts),
        out_shape=jax.ShapeDtypeStruct(
            (row_total, features), residual.dtype if last else jnp.float32
        ),
        in_specs=in_specs,
        out_specs=vmem_spec(),
        scratch_shapes=[
            VMEM((count, features, width), jnp.bfloat16),
            pltpu.SemaphoreType.DMA((count,)),
        ],
        compiler_params=pltpu.CompilerParams(vmem_limit_bytes=50 * MIB),
        cost_estimate=pl.CostEstimate(
            flops=2 * row_total * count * width * features,
            bytes_accessed=2 * count * width * features,
            transcendentals=0,
        ),
    )(*operands)


def attention_kernel(heads, lengths_ref, *refs):
    mixed_refs, refs = refs[:-9], refs[-9:]
    cosine_ref, sine_ref, query_gain_ref, key_gain_ref, keys_ref, values_ref = refs[:6]
    attended_ref, query_rows, result_rows = refs[6:]
    steps, rows, _ = mixed_refs[0].shape
    slots, size = keys_ref.shape[-2:]
    step_rows = steps * rows
    per_row = heads * steps
    first_row = pl.program_id(0) * rows
    scale = size ** (-0.5)
    cosine = cosine_ref[...]
    sine = sine_ref[...]

    def projected(vector):
        columns = slice(vector * size, (vector + 1) * size)
        return sum(ref[:, :, columns] for ref in mixed_refs)

    def turned(vectors, gain):
        mean = jnp.mean(vectors * vectors, axis=-1, keepdims=True)
        normal = vectors * lax.rsqrt(mean + epsilon) * gain
        swapped = jnp.concatenate([normal[..., size // 2 :], normal[..., : size // 2]], axis=-1)
        return normal * cosine + swapped * sine

    for head in range(heads):
        vectors = projected(head)
        query = turned(vectors, query_gain_ref[...])
        query_rows[head * step_rows : (head + 1) * step_rows, :] = query.reshape(step_rows, size)
    new_key = turned(projected(heads), key_gain_ref[...])
    new_key = new_key.reshape(step_rows, size).astype(jnp.bfloat16)
    new_value = projected(heads + 1)
    new_value = new_value.reshape(step_rows, size).astype(jnp.bfloat16)

    queries = [
        query_rows[pl.ds(r, per_row, stride=rows), :].astype(jnp.bfloat16) for r in range(rows)
    ]
    nt = (((1,), (1,)), ((), ()))
    column = lax.broadcasted_iota(jnp.int32, (per_row, slots), 1)
    old = []
    for r in range(rows):
        score = lax.dot_general(
            queries[r], keys_ref[r], nt, preferred_element_type=jnp.float32
        )
        old.append(jnp.where(column < lengths_ref[first_row + r], score * scale, -jnp.inf))
    old = jnp.concatenate(old, axis=0)
    new = lax.dot_general(
        jnp.concatenate(queries, axis=0), new_key, nt, preferred_element_type=jnp.float32
    )
    at = lax.broadcasted_iota(jnp.int32, (rows * per_row, step_rows), 0)
    to = lax.broadcasted_iota(jnp.int32, (rows * per_row, step_rows), 1)
    seen = (at // per_row == to % rows) & (to // rows <= at % steps)
    new = jnp.where(seen, new * scale, -jnp.inf)
    highest = jnp.maximum(
        jnp.max(old, axis=-1, keepdims=True), jnp.max(new, axis=-1, keepdims=True)
    )
    old = jnp.exp(old - highest)
    new = jnp.exp(new - highest)
    total = jnp.sum(old, axis=-1, keepdims=True) + jnp.sum(new, axis=-1, keepdims=True)
    old = (old / total).astype(jnp.bfloat16)
    new = (new / total).astype(jnp.bfloat16)
    from_new = jnp.dot(new, new_value, preferred_element_type=jnp.float32)
    for r in range(rows):
        part = slice(r * per_row, (r + 1) * per_row)
        result = jnp.dot(old[part], values_ref[r], preferred_element_type=jnp.float32)
        result_rows[pl.ds(r, per_row, stride=rows), :] = result + from_new[part]
    for head in range(heads):
        result = result_rows[head * step_rows : (head + 1) * step_rows, :]
        attended_ref[:, :, head * size : (head + 1) * size] = result.reshape(
            steps, rows, size
        ).astype(jnp.bfloat16)


def attend(mixed, cosine, sine, query_gain, key_gain, keys, values, lengths, layer):
    steps, row_total, columns = mixed[0].shape
    groups, slots, size = keys.shape[2:]
    per_group = columns // (groups * size)
    heads = per_group - 2
    rows = 16
    cache_spec = pl.BlockSpec(
        (None, rows, None, slots, size), lambda i, g, _: (layer, i, g, 0, 0)
    )
    turn_spec = pl.BlockSpec((steps, rows, size), lambda i, g, _: (0, i, 0))
    gain_spec = pl.BlockSpec((1, size), lambda i, g, _: (0, 0))
    return pl.pallas_call(
        functools.partial(attention_kernel, heads),
        out_shape=jax.ShapeDtypeStruct((steps, row_total, groups * heads * size), jnp.bfloat16),
        grid_spec=pltpu.PrefetchScalarGridSpec(
            num_scalar_prefetch=1,
            grid=(row_total // rows, groups),
            in_specs=[pl.BlockSpec((steps, rows, per_group * size), lambda i, g, _: (0, i, g))]
            * len(mixed)
            + [
                turn_spec,
                turn_spec,
                gain_spec,
                gain_spec,
                cache_spec,
                cache_spec,
            ],
            out_specs=pl.BlockSpec((steps, rows, heads * size), lambda i, g, _: (0, i, g)),
            scratch_shapes=[
                VMEM((heads * steps * rows, size), jnp.float32),
                VMEM((heads * steps * rows, size), jnp.float32),
            ],
        ),
        compiler_params=pltpu.CompilerParams(vmem_limit_bytes=49 * MIB),
        cost_estimate=pl.CostEstimate(
            flops=4 * row_total * groups * heads * steps * slots * size,
            bytes_accessed=4 * row_total * groups * slots * size,
            transcendentals=row_total * groups * heads * steps * slots,
        ),
    )(lengths, *mixed, cosine, sine, query_gain, key_gain, keys, values)


def on_device(
    inputs,
    qkv_weight,
    out_weight,
    norm_gain,
    query_gain,
    key_gain,
    stored_rotated_keys,
    stored_cache_values,
    lengths,
):
    step_count, row_count, model_width = inputs.shape
    flat_rows = step_count * row_count
    layers = qkv_weight.shape[0]
    head_dim = stored_rotated_keys.shape[4]
    parts = lax.axis_size("tp")
    replicas = lax.axis_size("rep")
    me = lax.axis_index("tp")
    piece = qkv_weight.shape[1]
    slice_width = replicas * piece
    block_width = qkv_weight.shape[2] // parts
    head_width = out_weight.shape[2] // parts
    merge = piece % 16 == 0

    def shifted(block, shift):
        if shift == 0:
            return block
        return lax.ppermute(block, "tp", [(i, (i + shift) % parts) for i in range(parts)])

    def all_parts(block, *earlier):
        if parts != 4:
            return [shifted(block, shift) for shift in range(parts)]
        one, three = shifted(block, 1), shifted(block, 3)
        from_left, from_right = one, three
        if earlier:
            from_left, from_right = lax.optimization_barrier((one, three) + earlier)[:2]
        rightwards = lax.ppermute(from_left, "tp", [(1, 2), (2, 3)])
        leftwards = lax.ppermute(from_right, "tp", [(1, 0), (2, 1)])
        return [block, one, jnp.where(me >= 2, rightwards, leftwards), three]

    def outgoing(layer, shift):
        target = lax.rem(me + shift, parts)
        return lax.dynamic_slice(
            qkv_weight, (layer, 0, target * block_width), (1, piece, block_width)
        )[0]

    source = lax.rem(me - jnp.arange(parts, dtype=jnp.int32) + parts, parts)
    seat = lax.axis_index("rep")
    by_links = merge and replicas == 8 and parts == 4 and layers == 2

    def after(array, *earlier):
        return lax.optimization_barrier((array,) + earlier)[0]

    def swapped(block, mask):
        return lax.ppermute(block, "rep", [(i, i ^ mask) for i in range(replicas)])

    def spread_first(block, *earlier):
        block = after(block, *earlier) if earlier else block
        return [(0, 0, block), (2, 0, swapped(block, 2)), (4, 0, swapped(block, 4))]

    def spread_second(spread):
        by_x, by_y = spread[1][2], spread[2][2]
        half = by_x.shape[0] // 2
        return spread + [(6, 0, swapped(by_x[:half], 4)), (6, half, swapped(by_y[half:], 2))]

    def listed(spreads, shifts):
        arrays, pieces, rows = [], [], []
        for spread, its_shifts in zip(spreads, shifts):
            for mask, first, array in spread:
                at = 0
                while at < array.shape[0]:
                    place, offset = divmod(first + at, piece)
                    count = min(piece - offset, array.shape[0] - at)
                    pieces.append((len(arrays), at, count, its_shifts[place]))
                    rows.append(((seat ^ mask) // 2) * piece + offset)
                    at += count
                arrays.append(array)
        return arrays, pieces, jnp.stack(rows).astype(jnp.int32)

    positions = lengths[None, :] + jnp.arange(step_count, dtype=jnp.int32)[:, None]
    half = head_dim // 2
    frequency = rope_base ** (-jnp.arange(half, dtype=jnp.float32) / half)
    angles = positions.astype(jnp.float32)[..., None] * frequency
    cosine, sine = jnp.cos(angles), jnp.sin(angles)
    cosine = jnp.concatenate([cosine, cosine], axis=-1)
    sine = jnp.concatenate([-sine, sine], axis=-1)

    gains = jnp.take(norm_gain.reshape(layers, replicas, parts, piece), source, axis=2)
    gains = jnp.moveaxis(gains, 2, 1).reshape(layers, parts, 1, slice_width)

    flat = inputs.reshape(flat_rows, model_width)
    blocks = split_parts(flat, source, parts, replicas, piece)
    hidden = [blocks[shift] for shift in range(parts)]

    def from_calls(layer):
        arrays = [
            lax.all_gather(shifted(outgoing(layer, shift), shift), "rep", axis=0, tiled=True)
            for shift in range(parts)
        ]
        pieces = [(shift, 0, slice_width, shift) for shift in range(parts)]
        return arrays, pieces, jnp.zeros((parts,), jnp.int32)

    def from_call(came):
        array = lax.all_gather(came, "rep", axis=0, tiled=True)
        pieces = [
            (0, (r * parts + shift) * piece, piece, shift)
            for r in range(replicas)
            for shift in range(parts)
        ]
        rows = jnp.array([r * piece for r in range(replicas) for _ in range(parts)], jnp.int32)
        return [array], pieces, rows

    stages = [[0, 1, 3], [2]]

    def row_scale(squares):
        return lax.rsqrt(squares / model_width + epsilon)

    if by_links:
        core = lax.rem(seat, 2)
        mine, theirs, squares = share_features(
            flat, jnp.full((1,), core, jnp.int32), replicas // 2
        )
        swapped_share = swapped(theirs, 1)
        both = jnp.concatenate([mine, swapped_share], axis=0)
        both = split_parts(both, source, parts, replicas // 2, piece)
        both = [both[shift] for shift in range(parts)]
        other = swapped(squares.reshape(-1, 128), 1).reshape(flat_rows, 1)
        scale = row_scale(jnp.concatenate([squares, other], axis=0))
        core_gains = lax.dynamic_index_in_dim(
            gains[0].reshape(parts, replicas // 2, 2, piece), core, 2, keepdims=False
        ).reshape(parts, 1, slice_width // 2)
        one, three = shifted(outgoing(0, 1), 1), shifted(outgoing(0, 3), 3)
        two = shifted(after(outgoing(0, 2), one, three, swapped_share), 2)
        head = spread_first(outgoing(0, 0))
        body = spread_first(
            jnp.concatenate([one, three], axis=0), head[1][2], head[2][2]
        )
        head = spread_second(head)
        turned = [array for _, _, array in head[3:5]]
        tail = spread_first(two, body[1][2], body[2][2], *turned)
        ahead = [array for _, _, array in body[1:3]]
        across = [array for _, _, array in tail[1:3]]
        body = spread_second(body)
        tail = spread_second(tail)
        gathers = [[listed([head, body], [[0], [1, 2]]), listed([tail], [[0]])]]
        later_one = shifted(after(outgoing(1, 1), two), 1)
        later_two = shifted(after(outgoing(1, 2), *across), 2)
        later_three = shifted(after(outgoing(1, 3), later_two), 3)
        came = (outgoing(1, 0), later_one, later_two, later_three)
        ready = (scale, core_gains, gathers[0][0][2], gathers[0][1][2], *both)
        sent = [after(out_weight[0], *ahead, *turned, two, *ready), out_weight[1]]
    else:
        gathers = [from_calls(layer) for layer in range(layers)]
        sent = [out_weight[layer] for layer in range(layers)]
    outs = [lax.all_gather(one, "rep", axis=0, tiled=True) for one in sent]

    columns = source * head_width
    for layer in range(layers):
        if by_links and layer == 0:
            mixed = None
            for stage, (arrays, pieces, rows) in zip(stages, gathers[0]):
                if mixed is not None:
                    mixed = lax.optimization_barrier(
                        (*mixed, later_one, later_two)
                    )[:2]
                mixed = project_qkv(
                    both, stage, core_gains, scale, arrays, pieces, rows, mixed, outputs=2
                )
            mixed = [mixed[0], swapped(mixed[1], 1)]
        else:
            mixed = project_qkv(
                hidden, list(range(parts)), gains[layer], None, *gathers[layer]
            )
        attended = attend(
            [one.reshape(step_count, row_count, block_width) for one in mixed],
            cosine,
            sine,
            query_gain[layer][None],
            key_gain[layer][None],
            stored_rotated_keys,
            stored_cache_values,
            lengths,
            layer,
        ).reshape(flat_rows, head_width)
        if by_links and layer == 0:
            came = lax.optimization_barrier((*came, attended))[:parts]
            gathers.append(from_call(jnp.concatenate(came, axis=0)))
            attended = all_parts(attended, outs[layer])
            own = project_out(attended, stages[0], outs[layer], columns)
            own = project_out(attended, stages[1], outs[layer], columns, own, hidden[0])
        else:
            own = project_out_whole(all_parts(attended), outs[layer], columns, hidden[0])
        hidden = all_parts(own)
    joined = join_parts(hidden, source, replicas, piece)
    return joined.reshape(step_count, row_count, model_width)


def solution(mesh):
    return jax.shard_map(
        on_device,
        mesh=mesh,
        in_specs=(
            P(None, "rep", None),
            P(None, ("rep", "tp"), None),
            P(None, ("rep", "tp"), None),
            P(),
            P(),
            P(),
            P(None, "rep", "tp", None, None),
            P(None, "rep", "tp", None, None),
            P("rep"),
        ),
        out_specs=P(None, "rep", None),
        check_vma=False,
    )
```

```python
import functools

import jax
import jax.numpy as jnp
from jax import lax
from jax.experimental import pallas as pl
from jax.experimental.pallas import tpu as pltpu
from jax.sharding import PartitionSpec as P

epsilon = 1e-06
rope_base = 1000000.0
MIB = 1024 * 1024
VMEM = pltpu.VMEM
SMEM = pltpu.SMEM


def vmem_spec():
    return pl.BlockSpec(memory_space=VMEM)


def smem_spec():
    return pl.BlockSpec(memory_space=SMEM)


def any_spec():
    return pl.BlockSpec(memory_space=pl.ANY)


def tiles(width, size=256):
    return [(start, min(size, width - start)) for start in range(0, width, size)]


def split_kernel(parts, replicas, piece, place_ref, whole_ref, blocks_ref):
    for part in range(parts):
        columns = [
            whole_ref[:, (r * parts + part) * piece : (r * parts + part + 1) * piece]
            for r in range(replicas)
        ]
        blocks_ref[place_ref[part]] = jnp.concatenate(columns, axis=1)


def split_parts(whole, place, parts, replicas, piece):
    rows = whole.shape[0]
    return pl.pallas_call(
        functools.partial(split_kernel, parts, replicas, piece),
        out_shape=jax.ShapeDtypeStruct((parts, rows, replicas * piece), whole.dtype),
        in_specs=[smem_spec(), vmem_spec()],
        out_specs=vmem_spec(),
        compiler_params=pltpu.CompilerParams(vmem_limit_bytes=24 * MIB),
    )(place, whole)


def share_kernel(shares, core_ref, whole_ref, mine_ref, theirs_ref, squares_ref):
    width = mine_ref.shape[1] // shares
    core = core_ref[0]
    squares = None
    for share in range(shares):
        columns = slice(share * width, (share + 1) * width)
        for whose, to_ref in ((core, mine_ref), (1 - core, theirs_ref)):
            start = pl.multiple_of((2 * share + whose) * width, 128)
            some = whole_ref[:, pl.ds(start, width)]
            to_ref[:, columns] = some
            wide = some.astype(jnp.float32)
            term = jnp.sum(wide * wide, axis=1, keepdims=True)
            squares = term if squares is None else squares + term
    squares_ref[...] = squares


def share_features(whole, core, shares):
    rows, width = whole.shape
    part = jax.ShapeDtypeStruct((rows, width // 2), whole.dtype)
    return pl.pallas_call(
        functools.partial(share_kernel, shares),
        out_shape=(part, part, jax.ShapeDtypeStruct((rows, 1), jnp.float32)),
        in_specs=[smem_spec(), vmem_spec()],
        out_specs=(vmem_spec(), vmem_spec(), vmem_spec()),
        compiler_params=pltpu.CompilerParams(vmem_limit_bytes=24 * MIB),
    )(core, whole)


def join_kernel(parts, replicas, piece, place_ref, *refs):
    block_refs, whole_ref, held, sems = refs[:parts], refs[parts], refs[parts + 1], refs[parts + 2]
    copies = [
        pltpu.make_async_copy(block_refs[shift], held.at[place_ref[shift]], sems.at[shift])
        for shift in range(parts)
    ]
    for copy in copies:
        copy.start()
    for copy in copies:
        copy.wait()
    for r in range(replicas):
        columns = [held[part, :, r * piece : (r + 1) * piece] for part in range(parts)]
        whole_ref[:, r * parts * piece : (r + 1) * parts * piece] = jnp.concatenate(columns, axis=1)


def join_parts(blocks, place, replicas, piece):
    parts = len(blocks)
    rows = blocks[0].shape[0]
    return pl.pallas_call(
        functools.partial(join_kernel, parts, replicas, piece),
        out_shape=jax.ShapeDtypeStruct((rows, parts * replicas * piece), blocks[0].dtype),
        in_specs=[smem_spec()] + [any_spec()] * parts,
        out_specs=vmem_spec(),
        scratch_shapes=[
            VMEM((parts, rows, replicas * piece), blocks[0].dtype),
            pltpu.SemaphoreType.DMA((parts,)),
        ],
        compiler_params=pltpu.CompilerParams(vmem_limit_bytes=24 * MIB),
    )(place, *blocks)


def qkv_kernel(count, shifts, pieces, arrays, scaled, continued, rows_ref, *refs):
    block_refs, refs = refs[:count], refs[count:]
    gain_ref, refs = refs[0], refs[1:]
    if scaled:
        scale_ref, refs = refs[0], refs[1:]
    weight_refs, refs = refs[:arrays], refs[arrays:]
    outputs = (len(refs) - 3) // (2 if continued else 1)
    if continued:
        before_refs, refs = refs[:outputs], refs[outputs:]
    mixed_refs, refs = refs[:outputs], refs[outputs:]
    held, normed, sems = refs
    each = mixed_refs[0].shape[0]
    copies = []
    for index, (array, first, size, place) in enumerate(pieces):
        to = pl.multiple_of(rows_ref[index], 16)
        copies.append(
            pltpu.make_async_copy(
                weight_refs[array].at[pl.ds(first, size)],
                held.at[place, pl.ds(to, size)],
                sems.at[index],
            )
        )
        copies[-1].start()
    step = 32

    @pl.loop(0, normed.shape[1] // step)
    def _(tile):
        rows = pl.ds(pl.multiple_of(tile * step, step), step)
        if scaled:
            scale = scale_ref[rows, :]
        else:
            squares = None
            for ref in block_refs:
                wide = ref[rows, :].astype(jnp.float32)
                term = jnp.sum(wide * wide, axis=-1, keepdims=True)
                squares = term if squares is None else squares + term
            scale = lax.rsqrt(squares / (count * normed.shape[2]) + epsilon)
        for place, shift in enumerate(shifts):
            wide = block_refs[place][rows, :].astype(jnp.float32)
            normed[place, rows, :] = (wide * scale * gain_ref[shift]).astype(jnp.bfloat16)

    for place in range(count):
        for index in range(len(pieces)):
            if pieces[index][3] == place:
                copies[index].wait()
        for start, size in tiles(mixed_refs[0].shape[1]):
            columns = slice(start, start + size)
            terms = jnp.dot(
                normed[place], held[place, :, columns], preferred_element_type=jnp.float32
            )
            for index in range(outputs):
                term = terms[index * each : (index + 1) * each]
                if place > 0:
                    mixed_refs[index][:, columns] += term
                elif continued:
                    mixed_refs[index][:, columns] = before_refs[index][:, columns] + term
                else:
                    mixed_refs[index][:, columns] = term


def project_qkv(
    blocks, shifts, gains, scale, weights, pieces, rows, before=None, outputs=1
):
    count = len(shifts)
    row_total, width = blocks[0].shape
    columns = weights[0].shape[1]
    continued = before is not None
    scaled = scale is not None
    operands = [rows] + [blocks[shift] for shift in shifts] + [gains] + [scale] * scaled
    in_specs = [smem_spec()] + [vmem_spec()] * (len(operands) - 1) + [any_spec()] * len(weights)
    operands += list(weights)
    if continued:
        operands += list(before)
        in_specs += [vmem_spec()] * outputs
    mixed = jax.ShapeDtypeStruct((row_total // outputs, columns), jnp.float32)
    return pl.pallas_call(
        functools.partial(
            qkv_kernel, count, shifts, pieces, len(weights), scaled, continued
        ),
        out_shape=[mixed] * outputs,
        in_specs=in_specs,
        out_specs=[vmem_spec()] * outputs,
        scratch_shapes=[
            VMEM((count, width, columns), jnp.bfloat16),
            VMEM((count, row_total, width), jnp.bfloat16),
            pltpu.SemaphoreType.DMA((len(pieces),)),
        ],
        compiler_params=pltpu.CompilerParams(vmem_limit_bytes=(52 if scaled else 40) * MIB),
        cost_estimate=pl.CostEstimate(
            flops=2 * row_total * count * width * columns,
            bytes_accessed=2 * count * width * columns,
            transcendentals=0,
        ),
    )(*operands)


def whole_out_kernel(count, column_ref, *refs):
    attended_refs, refs = refs[:count], refs[count:]
    weight_ref, residual_ref, hidden_ref, held, total, sems = refs
    width = attended_refs[0].shape[1]
    copies = []
    for shift in range(count):
        start = pl.multiple_of(column_ref[shift], 128)
        copies.append(
            pltpu.make_async_copy(
                weight_ref.at[:, pl.ds(start, width)], held.at[shift], sems.at[shift]
            )
        )
        copies[-1].start()
    for shift in range(count):
        copies[shift].wait()
        for start, size in tiles(hidden_ref.shape[1]):
            features = slice(start, start + size)
            term = lax.dot_general(
                attended_refs[shift][...],
                held[shift, features, :],
                (((1,), (1,)), ((), ())),
                preferred_element_type=jnp.float32,
            )
            if shift > 0:
                term = total[:, features] + term
            if shift < count - 1:
                total[:, features] = term
            else:
                hidden_ref[:, features] = (
                    residual_ref[:, features].astype(jnp.float32) + term
                ).astype(hidden_ref.dtype)


def project_out_whole(attended, weight, columns, residual):
    count = len(attended)
    row_total, width = attended[0].shape
    features = weight.shape[0]
    return pl.pallas_call(
        functools.partial(whole_out_kernel, count),
        out_shape=jax.ShapeDtypeStruct((row_total, features), residual.dtype),
        in_specs=[smem_spec()] + [vmem_spec()] * count + [any_spec(), vmem_spec()],
        out_specs=vmem_spec(),
        scratch_shapes=[
            VMEM((count, features, width), jnp.bfloat16),
            VMEM((row_total, features), jnp.float32),
            pltpu.SemaphoreType.DMA((count,)),
        ],
        compiler_params=pltpu.CompilerParams(vmem_limit_bytes=50 * MIB),
        cost_estimate=pl.CostEstimate(
            flops=2 * row_total * count * width * features,
            bytes_accessed=2 * count * width * features,
            transcendentals=0,
        ),
    )(columns, *attended, weight, residual)


def out_kernel(count, shifts, column_ref, *refs):
    attended_refs, refs = refs[:count], refs[count:]
    weight_ref, refs = refs[0], refs[1:]
    last = len(refs) > 3
    if last:
        before_ref, residual_ref, refs = refs[0], refs[1], refs[2:]
    sum_ref, held, sems = refs[0], refs[-2], refs[-1]
    width = attended_refs[0].shape[1]
    copies = []
    for place, shift in enumerate(shifts):
        start = pl.multiple_of(column_ref[shift], 128)
        copies.append(
            pltpu.make_async_copy(
                weight_ref.at[:, pl.ds(start, width)], held.at[place], sems.at[place]
            )
        )
        copies[-1].start()
    for place in range(count):
        copies[place].wait()
        for start, size in tiles(sum_ref.shape[1]):
            features = slice(start, start + size)
            term = lax.dot_general(
                attended_refs[place][...],
                held[place, features, :],
                (((1,), (1,)), ((), ())),
                preferred_element_type=jnp.float32,
            )
            if last:
                total = before_ref[:, features] + term
                total = residual_ref[:, features].astype(jnp.float32) + total
                sum_ref[:, features] = total.astype(sum_ref.dtype)
            elif place > 0:
                sum_ref[:, features] += term
            else:
                sum_ref[:, features] = term


def project_out(attended, shifts, weight, columns, before=None, residual=None):
    count = len(shifts)
    row_total, width = attended[0].shape
    features = weight.shape[0]
    last = residual is not None
    operands = [columns] + [attended[shift] for shift in shifts] + [weight]
    in_specs = [smem_spec()] + [vmem_spec()] * count + [any_spec()]
    if last:
        operands += [before, residual]
        in_specs += [vmem_spec()] * 2
    return pl.pallas_call(
        functools.partial(out_kernel, count, shifts),
        out_shape=jax.ShapeDtypeStruct(
            (row_total, features), residual.dtype if last else jnp.float32
        ),
        in_specs=in_specs,
        out_specs=vmem_spec(),
        scratch_shapes=[
            VMEM((count, features, width), jnp.bfloat16),
            pltpu.SemaphoreType.DMA((count,)),
        ],
        compiler_params=pltpu.CompilerParams(vmem_limit_bytes=50 * MIB),
        cost_estimate=pl.CostEstimate(
            flops=2 * row_total * count * width * features,
            bytes_accessed=2 * count * width * features,
            transcendentals=0,
        ),
    )(*operands)


def attention_kernel(heads, lengths_ref, *refs):
    mixed_refs, refs = refs[:-9], refs[-9:]
    cosine_ref, sine_ref, query_gain_ref, key_gain_ref, keys_ref, values_ref = refs[:6]
    attended_ref, query_rows, result_rows = refs[6:]
    steps, rows, _ = mixed_refs[0].shape
    slots, size = keys_ref.shape[-2:]
    step_rows = steps * rows
    per_row = heads * steps
    first_row = pl.program_id(0) * rows
    scale = size ** (-0.5)
    cosine = cosine_ref[...]
    sine = sine_ref[...]

    def projected(vector):
        columns = slice(vector * size, (vector + 1) * size)
        return sum(ref[:, :, columns] for ref in mixed_refs)

    def turned(vectors, gain):
        mean = jnp.mean(vectors * vectors, axis=-1, keepdims=True)
        normal = vectors * lax.rsqrt(mean + epsilon) * gain
        swapped = jnp.concatenate([normal[..., size // 2 :], normal[..., : size // 2]], axis=-1)
        return normal * cosine + swapped * sine

    for head in range(heads):
        vectors = projected(head)
        query = turned(vectors, query_gain_ref[...])
        query_rows[head * step_rows : (head + 1) * step_rows, :] = query.reshape(step_rows, size)
    new_key = turned(projected(heads), key_gain_ref[...])
    new_key = new_key.reshape(step_rows, size).astype(jnp.bfloat16)
    new_value = projected(heads + 1)
    new_value = new_value.reshape(step_rows, size).astype(jnp.bfloat16)

    queries = [
        query_rows[pl.ds(r, per_row, stride=rows), :].astype(jnp.bfloat16) for r in range(rows)
    ]
    nt = (((1,), (1,)), ((), ()))
    column = lax.broadcasted_iota(jnp.int32, (per_row, slots), 1)
    old = []
    for r in range(rows):
        score = lax.dot_general(
            queries[r], keys_ref[r], nt, preferred_element_type=jnp.float32
        )
        old.append(jnp.where(column < lengths_ref[first_row + r], score * scale, -jnp.inf))
    old = jnp.concatenate(old, axis=0)
    new = lax.dot_general(
        jnp.concatenate(queries, axis=0), new_key, nt, preferred_element_type=jnp.float32
    )
    at = lax.broadcasted_iota(jnp.int32, (rows * per_row, step_rows), 0)
    to = lax.broadcasted_iota(jnp.int32, (rows * per_row, step_rows), 1)
    seen = (at // per_row == to % rows) & (to // rows <= at % steps)
    new = jnp.where(seen, new * scale, -jnp.inf)
    highest = jnp.maximum(
        jnp.max(old, axis=-1, keepdims=True), jnp.max(new, axis=-1, keepdims=True)
    )
    old = jnp.exp(old - highest)
    new = jnp.exp(new - highest)
    total = jnp.sum(old, axis=-1, keepdims=True) + jnp.sum(new, axis=-1, keepdims=True)
    old = (old / total).astype(jnp.bfloat16)
    new = (new / total).astype(jnp.bfloat16)
    from_new = jnp.dot(new, new_value, preferred_element_type=jnp.float32)
    for r in range(rows):
        part = slice(r * per_row, (r + 1) * per_row)
        result = jnp.dot(old[part], values_ref[r], preferred_element_type=jnp.float32)
        result_rows[pl.ds(r, per_row, stride=rows), :] = result + from_new[part]
    for head in range(heads):
        result = result_rows[head * step_rows : (head + 1) * step_rows, :]
        attended_ref[:, :, head * size : (head + 1) * size] = result.reshape(
            steps, rows, size
        ).astype(jnp.bfloat16)


def attend(mixed, cosine, sine, query_gain, key_gain, keys, values, lengths, layer):
    steps, row_total, columns = mixed[0].shape
    groups, slots, size = keys.shape[2:]
    per_group = columns // (groups * size)
    heads = per_group - 2
    rows = 16
    cache_spec = pl.BlockSpec(
        (None, rows, None, slots, size), lambda i, g, _: (layer, i, g, 0, 0)
    )
    turn_spec = pl.BlockSpec((steps, rows, size), lambda i, g, _: (0, i, 0))
    gain_spec = pl.BlockSpec((1, size), lambda i, g, _: (0, 0))
    return pl.pallas_call(
        functools.partial(attention_kernel, heads),
        out_shape=jax.ShapeDtypeStruct((steps, row_total, groups * heads * size), jnp.bfloat16),
        grid_spec=pltpu.PrefetchScalarGridSpec(
            num_scalar_prefetch=1,
            grid=(row_total // rows, groups),
            in_specs=[pl.BlockSpec((steps, rows, per_group * size), lambda i, g, _: (0, i, g))]
            * len(mixed)
            + [
                turn_spec,
                turn_spec,
                gain_spec,
                gain_spec,
                cache_spec,
                cache_spec,
            ],
            out_specs=pl.BlockSpec((steps, rows, heads * size), lambda i, g, _: (0, i, g)),
            scratch_shapes=[
                VMEM((heads * steps * rows, size), jnp.float32),
                VMEM((heads * steps * rows, size), jnp.float32),
            ],
        ),
        compiler_params=pltpu.CompilerParams(vmem_limit_bytes=49 * MIB),
        cost_estimate=pl.CostEstimate(
            flops=4 * row_total * groups * heads * steps * slots * size,
            bytes_accessed=4 * row_total * groups * slots * size,
            transcendentals=row_total * groups * heads * steps * slots,
        ),
    )(lengths, *mixed, cosine, sine, query_gain, key_gain, keys, values)


def on_device(
    inputs,
    qkv_weight,
    out_weight,
    norm_gain,
    query_gain,
    key_gain,
    stored_rotated_keys,
    stored_cache_values,
    lengths,
):
    step_count, row_count, model_width = inputs.shape
    flat_rows = step_count * row_count
    layers = qkv_weight.shape[0]
    head_dim = stored_rotated_keys.shape[4]
    parts = lax.axis_size("tp")
    replicas = lax.axis_size("rep")
    me = lax.axis_index("tp")
    piece = qkv_weight.shape[1]
    slice_width = replicas * piece
    block_width = qkv_weight.shape[2] // parts
    head_width = out_weight.shape[2] // parts
    merge = piece % 16 == 0

    def shifted(block, shift):
        if shift == 0:
            return block
        return lax.ppermute(block, "tp", [(i, (i + shift) % parts) for i in range(parts)])

    def all_parts(block, *earlier):
        if parts != 4:
            return [shifted(block, shift) for shift in range(parts)]
        one, three = shifted(block, 1), shifted(block, 3)
        from_left, from_right = one, three
        if earlier:
            from_left, from_right = lax.optimization_barrier((one, three) + earlier)[:2]
        rightwards = lax.ppermute(from_left, "tp", [(1, 2), (2, 3)])
        leftwards = lax.ppermute(from_right, "tp", [(1, 0), (2, 1)])
        return [block, one, jnp.where(me >= 2, rightwards, leftwards), three]

    def outgoing(layer, shift):
        target = lax.rem(me + shift, parts)
        return lax.dynamic_slice(
            qkv_weight, (layer, 0, target * block_width), (1, piece, block_width)
        )[0]

    source = lax.rem(me - jnp.arange(parts, dtype=jnp.int32) + parts, parts)
    seat = lax.axis_index("rep")
    by_links = merge and replicas == 8 and parts == 4 and layers == 2

    def after(array, *earlier):
        return lax.optimization_barrier((array,) + earlier)[0]

    def swapped(block, mask):
        return lax.ppermute(block, "rep", [(i, i ^ mask) for i in range(replicas)])

    def spread_first(block, *earlier):
        block = after(block, *earlier) if earlier else block
        return [(0, 0, block), (2, 0, swapped(block, 2)), (4, 0, swapped(block, 4))]

    def spread_second(spread):
        by_x, by_y = spread[1][2], spread[2][2]
        half = by_x.shape[0] // 2
        return spread + [(6, 0, swapped(by_x[:half], 4)), (6, half, swapped(by_y[half:], 2))]

    def listed(spreads, shifts):
        arrays, pieces, rows = [], [], []
        for spread, its_shifts in zip(spreads, shifts):
            for mask, first, array in spread:
                at = 0
                while at < array.shape[0]:
                    place, offset = divmod(first + at, piece)
                    count = min(piece - offset, array.shape[0] - at)
                    pieces.append((len(arrays), at, count, its_shifts[place]))
                    rows.append(((seat ^ mask) // 2) * piece + offset)
                    at += count
                arrays.append(array)
        return arrays, pieces, jnp.stack(rows).astype(jnp.int32)

    positions = lengths[None, :] + jnp.arange(step_count, dtype=jnp.int32)[:, None]
    half = head_dim // 2
    frequency = rope_base ** (-jnp.arange(half, dtype=jnp.float32) / half)
    angles = positions.astype(jnp.float32)[..., None] * frequency
    cosine, sine = jnp.cos(angles), jnp.sin(angles)
    cosine = jnp.concatenate([cosine, cosine], axis=-1)
    sine = jnp.concatenate([-sine, sine], axis=-1)

    gains = jnp.take(norm_gain.reshape(layers, replicas, parts, piece), source, axis=2)
    gains = jnp.moveaxis(gains, 2, 1).reshape(layers, parts, 1, slice_width)

    flat = inputs.reshape(flat_rows, model_width)
    blocks = split_parts(flat, source, parts, replicas, piece)
    hidden = [blocks[shift] for shift in range(parts)]

    def from_calls(layer):
        arrays = [
            lax.all_gather(shifted(outgoing(layer, shift), shift), "rep", axis=0, tiled=True)
            for shift in range(parts)
        ]
        pieces = [(shift, 0, slice_width, shift) for shift in range(parts)]
        return arrays, pieces, jnp.zeros((parts,), jnp.int32)

    def from_call(came):
        array = lax.all_gather(came, "rep", axis=0, tiled=True)
        pieces = [
            (0, (r * parts + shift) * piece, piece, shift)
            for r in range(replicas)
            for shift in range(parts)
        ]
        rows = jnp.array([r * piece for r in range(replicas) for _ in range(parts)], jnp.int32)
        return [array], pieces, rows

    stages = [[0, 1, 3], [2]]

    def row_scale(squares):
        return lax.rsqrt(squares / model_width + epsilon)

    if by_links:
        core = lax.rem(seat, 2)
        mine, theirs, squares = share_features(
            flat, jnp.full((1,), core, jnp.int32), replicas // 2
        )
        swapped_share = swapped(theirs, 1)
        both = jnp.concatenate([mine, swapped_share], axis=0)
        both = split_parts(both, source, parts, replicas // 2, piece)
        both = [both[shift] for shift in range(parts)]
        other = swapped(squares.reshape(-1, 128), 1).reshape(flat_rows, 1)
        scale = row_scale(jnp.concatenate([squares, other], axis=0))
        core_gains = lax.dynamic_index_in_dim(
            gains[0].reshape(parts, replicas // 2, 2, piece), core, 2, keepdims=False
        ).reshape(parts, 1, slice_width // 2)
        one, three = shifted(outgoing(0, 1), 1), shifted(outgoing(0, 3), 3)
        two = shifted(after(outgoing(0, 2), one, three, swapped_share), 2)
        head = spread_first(outgoing(0, 0))
        body = spread_first(
            jnp.concatenate([one, three], axis=0), head[1][2], head[2][2]
        )
        head = spread_second(head)
        turned = [array for _, _, array in head[3:5]]
        tail = spread_first(two, body[1][2], body[2][2], *turned)
        ahead = [array for _, _, array in body[1:3]]
        across = [array for _, _, array in tail[1:3]]
        body = spread_second(body)
        turned += [array for _, _, array in body[3:5]]
        tail = spread_second(tail)
        gathers = [[listed([head, body], [[0], [1, 2]]), listed([tail], [[0]])]]
        later_one = shifted(after(outgoing(1, 1), two), 1)
        later_two = shifted(after(outgoing(1, 2), *across), 2)
        later_three = shifted(after(outgoing(1, 3), later_two), 3)
        came = (outgoing(1, 0), later_one, later_two, later_three)
        ready = (scale, core_gains, gathers[0][0][2], gathers[0][1][2], *both)
        sent = [after(out_weight[0], *across, *turned, later_one, *ready), out_weight[1]]
    else:
        gathers = [from_calls(layer) for layer in range(layers)]
        sent = [out_weight[layer] for layer in range(layers)]
    outs = [lax.all_gather(one, "rep", axis=0, tiled=True) for one in sent]

    columns = source * head_width
    for layer in range(layers):
        if by_links and layer == 0:
            mixed = None
            for stage, (arrays, pieces, rows) in zip(stages, gathers[0]):
                if mixed is not None:
                    mixed = lax.optimization_barrier(
                        (*mixed, later_one, later_two)
                    )[:2]
                mixed = project_qkv(
                    both, stage, core_gains, scale, arrays, pieces, rows, mixed, outputs=2
                )
            mixed = [mixed[0], swapped(mixed[1], 1)]
        else:
            mixed = project_qkv(
                hidden, list(range(parts)), gains[layer], None, *gathers[layer]
            )
        attended = attend(
            [one.reshape(step_count, row_count, block_width) for one in mixed],
            cosine,
            sine,
            query_gain[layer][None],
            key_gain[layer][None],
            stored_rotated_keys,
            stored_cache_values,
            lengths,
            layer,
        ).reshape(flat_rows, head_width)
        if by_links and layer == 0:
            came = lax.optimization_barrier((*came, attended))[:parts]
            gathers.append(from_call(jnp.concatenate(came, axis=0)))
            attended = all_parts(attended, outs[layer])
            own = project_out(attended, stages[0], outs[layer], columns)
            own = project_out(attended, stages[1], outs[layer], columns, own, hidden[0])
        else:
            own = project_out_whole(all_parts(attended), outs[layer], columns, hidden[0])
        hidden = all_parts(own)
    joined = join_parts(hidden, source, replicas, piece)
    return joined.reshape(step_count, row_count, model_width)


def solution(mesh):
    return jax.shard_map(
        on_device,
        mesh=mesh,
        in_specs=(
            P(None, "rep", None),
            P(None, ("rep", "tp"), None),
            P(None, ("rep", "tp"), None),
            P(),
            P(),
            P(),
            P(None, "rep", "tp", None, None),
            P(None, "rep", "tp", None, None),
            P("rep"),
        ),
        out_specs=P(None, "rep", None),
        check_vma=False,
    )
```
